32 devices in a mesh: group: 16 (over z, y, core), dp: 2 (over x).
Axes of the slice: x: 2, y: 2, z: 4, core: 2. Of those that a mesh axis runs over, the one named last changes fastest.
Arguments:
- tokens: bfloat16 [4096, 3584], P(('group', 'dp')), may hold values from -6 to 6
- routes: int32 [4096, 1], P(('group', 'dp')), may hold values from 0 to 7; in each aligned block of 128 rows (0 to 127, 128 to 255, ...) at most 24 rows name the same one
- gate_scale: float32 [4096, 1], P(('group', 'dp')), may hold values from 0.1 to 1
- cotangent: bfloat16 [4096, 3584], P(('group', 'dp')), may hold values from -0.59765625 to 0.59765625
- master: float32 [16, 512, 10752], P('group', 'dp'), may hold values from -0.09375 to 0.09375
- moment_one: float32 [16, 512, 10752], P('group', 'dp'), may hold values from -3 to 3
- moment_two: float32 [16, 512, 10752], P('group', 'dp'), may hold values from 0.01 to 1
- dec_tokens: bfloat16 [4, 256, 3584], P(None, 'group'), may hold values from -6 to 6
- dec_routes: int32 [4, 256, 1], P(None, 'group'), may hold values from 0 to 7; in each aligned block of 16 rows (0 to 15, 16 to 31, ..., all dimensions but the last counted through in order) at most 4 rows name the same one
- dec_scale: float32 [4, 256, 1], P(None, 'group'), may hold values from 0.5 to 2
Outputs:
- new_master: float32 [16, 512, 10752], P('group', 'dp')
- new_moment_one: float32 [16, 512, 10752], P('group', 'dp')
- new_moment_two: float32 [16, 512, 10752], P('group', 'dp')
- dec_out: bfloat16 [4, 256, 3584], P(None, 'group', 'dp')
The draws below stay inside these ranges and needn't reach their ends.
Inputs may be any that keep to these rules, and one draw needn't show every extreme that they name: `routes`: in each aligned block of 128 rows (the rows of one device) no expert is named by more than 24 rows; in some blocks one expert is named by exactly 24. `dec_routes`: within one step, in each aligned block of 16 rows (the rows of one index of group) no expert is named by more than 4 rows; in some blocks one expert is named by exactly 4.
All inputs are finite; a program needn't handle non-finite values.
Results may differ from the reference program's by a relative error of at most 0.0076.
Values may be sent and summed in bfloat16 or wider, within the bound.
A program may use at most 192 MiB of HBM per device.

```python
import math
import jax
import jax.numpy as jnp
import numpy as np
from jax import lax

D = 3584
EXPERTS = 8
STEPS = 4
TOK_DEV = 128
DEC_DEV = 16
FF_SLICE = 512
CAP = 24
DCAP = 4
TOKENS = 4096
DEC_ROWS = 256
N_GROUP = 16
N_DP = 2


def levels(key, shape, shards, smallest, top_value):
    level = 1.0
    for axis_at, blocks in shards:
        heights = jax.random.uniform(jax.random.fold_in(jax.random.fold_in(key, 6), axis_at), (blocks,), jnp.float32, smallest / len(shards), top_value / len(shards))
        level = level * jnp.repeat(jnp.exp(heights), shape[axis_at] // blocks).reshape((-1,) + (1,) * (len(shape) - 1 - axis_at))
    return level


def deal_out(stream_key, own, number, rows, amount, top, limit, slope):
    sequence = jax.random.permutation(stream_key, amount)
    packed, usual = load_shares(amount, rows * top, limit, slope, True), load_shares(amount, rows * top, limit, slope, False)
    places = jnp.arange(amount)

    def named(lengths, rotation):
        used = int((lengths > 0).sum())
        fixed = max(1, used // 4)
        passed = fixed + (places - fixed + rotation * (used - fixed)) % max(1, amount - fixed)
        return jnp.zeros((amount,), jnp.int32).at[sequence[jnp.where(places < fixed, places, passed)]].set(jnp.asarray(lengths, jnp.int32))

    lengths = jnp.where(number % 4 == 0, named(packed, number // 4), named(usual, number - number // 4 - 1))
    mixed = jax.random.permutation(jax.random.fold_in(own, 3), amount)
    giver, receiver = mixed[0:amount // 2 * 2:2], mixed[1:amount // 2 * 2:2]
    room = jnp.minimum(lengths[giver] - 1, limit - lengths[receiver]) // 2
    room = jnp.where((giver == sequence[0]) | (receiver == sequence[0]) | (lengths[receiver] == 0), 0, jnp.maximum(room, 0))
    passed = jax.random.randint(jax.random.fold_in(own, 4), (amount // 2,), 0, 1 << 20) % (room + 1)
    lengths = lengths.at[giver].add(-passed).at[receiver].add(passed)
    items = jnp.searchsorted(jnp.cumsum(lengths), jnp.arange(rows * top), side="right").astype(jnp.int32)
    table = items.reshape(top, rows).T
    table = table[jax.random.permutation(jax.random.fold_in(own, 1), rows)]
    rotation = jax.random.randint(jax.random.fold_in(own, 2), (rows, 1), 0, top)
    return jnp.take_along_axis(table, (jnp.arange(top)[None, :] + rotation) % top, axis=1)


def load_shares(number_of, total, bound, lean, full):
    portions = [(1 << 20) // math.isqrt(standing ** lean) + 1 for standing in range(1, number_of + 1)]
    largest = bound if full else min(bound, max(-(-total // number_of), total * portions[0] // sum(portions)))
    least = 1 if total - largest >= number_of - 1 else 0
    given, spare = [largest] + [least] * (number_of - 1), total - largest - least * (number_of - 1)
    while spare > 0:
        free = [i for i in range(1, number_of) if given[i] < largest] or [i for i in range(1, number_of) if given[i] < bound]
        mass, budget = sum([portions[i] for i in free]), spare
        for i in free:
            addition = min(bound - given[i], max(1, budget * portions[i] // mass), spare)
            given[i] = given[i] + addition
            spare = spare - addition
    return np.array(given)


def gaussian(rng, shape, width, limit, pieces=(), held_as=jnp.bfloat16):
    level = levels(rng, shape, pieces, -0.22, 0.18) if pieces else 1.0
    values = jax.random.normal(rng, shape, jnp.float32) * width * level
    return jnp.minimum(jnp.maximum(values, -limit), limit).astype(held_as)


def setup_inputs(seed: int = 0) -> dict:
    key_of = jax.random.split(jax.random.key(seed), 11)
    tokens = gaussian(key_of[0], (TOKENS, D), 1.0, 6.0, ((0, 32),))
    routes_keys = jax.random.split(jax.random.fold_in(key_of[1], 1), TOKENS // TOK_DEV)
    routes_turns = jax.random.permutation(jax.random.fold_in(key_of[1], 3), TOKENS // TOK_DEV)
    routes = jax.vmap(lambda own, number: deal_out(jax.random.fold_in(key_of[1], 2), own, number, TOK_DEV, EXPERTS, 1, CAP, 2))(routes_keys, routes_turns).reshape((TOKENS, 1))
    gate_scale = jnp.clip(jnp.exp(math.log(1.0) - 2.3025851 * jax.random.uniform(key_of[2], (TOKENS, 1), jnp.float32) ** levels(key_of[2], (TOKENS, 1), ((0, 32),), -0.2, 0.2)), 0.1, 1.0)
    cotangent = gaussian(key_of[3], (TOKENS, D), 0.1, 0.59765625, ((0, 32),))
    master = gaussian(key_of[4], (N_GROUP, FF_SLICE, 3 * D), D ** -0.5, 0.09375, ((0, 16), (1, 2)), jnp.float32)
    moment_one = gaussian(key_of[5], (N_GROUP, FF_SLICE, 3 * D), 0.5, 3.0, ((0, 16), (1, 2)), jnp.float32)
    moment_two = jnp.clip(jnp.exp(math.log(1.0) - 4.6051702 * jax.random.uniform(key_of[6], (N_GROUP, FF_SLICE, 3 * D), jnp.float32) ** levels(key_of[6], (N_GROUP, FF_SLICE, 3 * D), ((0, 16), (1, 2)), -0.2, 0.2)), 0.01, 1.0)
    dec_tokens = gaussian(key_of[7], (STEPS, DEC_ROWS, D), 1.0, 6.0, ((1, 16),))
    dec_routes_keys = jax.random.split(jax.random.fold_in(key_of[8], 1), STEPS * DEC_ROWS // DEC_DEV)
    dec_routes_turns = jax.random.permutation(jax.random.fold_in(key_of[8], 3), STEPS * DEC_ROWS // DEC_DEV)
    dec_routes = jax.vmap(lambda own, number: deal_out(jax.random.fold_in(key_of[8], 2), own, number, DEC_DEV, EXPERTS, 1, DCAP, 2))(dec_routes_keys, dec_routes_turns).reshape((STEPS, DEC_ROWS, 1))
    dec_scale = jnp.clip(jnp.exp(math.log(2.0) - 1.3862944 * jax.random.uniform(key_of[9], (STEPS, DEC_ROWS, 1), jnp.float32) ** levels(key_of[9], (STEPS, DEC_ROWS, 1), ((1, 16),), -0.2, 0.2)), 0.5, 2.0)
    return {"tokens": tokens, "routes": routes, "gate_scale": gate_scale, "cotangent": cotangent, "master": master, "moment_one": moment_one, "moment_two": moment_two, "dec_tokens": dec_tokens, "dec_routes": dec_routes, "dec_scale": dec_scale}


adam_lr = 0.001
beta_one = 0.9
beta_two = 0.95
adam_eps = 1e-08
decay_rate = 0.1
step_count = 100.0

def silu_parts(values):
    sig = jax.nn.sigmoid(values)
    return (values * sig, sig * (1.0 + values * (1.0 - sig)))

def by_expert(array):
    split = N_GROUP // EXPERTS
    shaped = array.reshape(split, EXPERTS, FF_SLICE, 3 * D)
    return jnp.transpose(shaped, (1, 0, 2, 3)).reshape(EXPERTS, split * FF_SLICE, 3 * D)

def reference(tokens, routes, gate_scale, cotangent, master, moment_one, moment_two, dec_tokens, dec_routes, dec_scale):
    split = N_GROUP // EXPERTS
    scaled = (gate_scale * cotangent.astype(jnp.float32)).astype(jnp.bfloat16)
    route_ids = routes[:, 0]
    total_cap = CAP * N_GROUP * N_DP
    expert_weights = by_expert(master.astype(jnp.bfloat16))

    def one_expert(expert):
        chosen = route_ids == expert
        index = jnp.nonzero(chosen, size=total_cap, fill_value=0)[0]
        valid = jnp.arange(total_cap) < jnp.sum(chosen.astype(jnp.int32))
        x_rows = jnp.where(valid[:, None], tokens[index], jnp.zeros((), jnp.bfloat16))
        d_rows = jnp.where(valid[:, None], scaled[index], jnp.zeros((), jnp.bfloat16))
        w_exp = lax.dynamic_index_in_dim(expert_weights, expert, 0, keepdims=False)
        gate_pre = jnp.dot(x_rows, w_exp[:, :D].T, preferred_element_type=jnp.float32)
        up_pre = jnp.dot(x_rows, w_exp[:, D:2 * D].T, preferred_element_type=jnp.float32)
        back_pre = jnp.dot(d_rows, w_exp[:, 2 * D:].T, preferred_element_type=jnp.float32)
        silu_val, silu_grad = silu_parts(gate_pre)
        activated = (silu_val * up_pre).astype(jnp.bfloat16)
        grad_up = (back_pre * silu_val).astype(jnp.bfloat16)
        grad_gate = (back_pre * up_pre * silu_grad).astype(jnp.bfloat16)
        return jnp.concatenate([jnp.dot(grad_gate.T, x_rows, preferred_element_type=jnp.float32), jnp.dot(grad_up.T, x_rows, preferred_element_type=jnp.float32), jnp.dot(activated.T, d_rows, preferred_element_type=jnp.float32)], axis=1)
    per_expert = lax.map(one_expert, jnp.arange(EXPERTS, dtype=jnp.int32))
    grads = jnp.transpose(per_expert.reshape(EXPERTS, split, FF_SLICE, 3 * D), (1, 0, 2, 3)).reshape(N_GROUP, FF_SLICE, 3 * D)
    new_moment_one = beta_one * moment_one + (1.0 - beta_one) * grads
    new_moment_two = beta_two * moment_two + (1.0 - beta_two) * grads * grads
    correct_one = 1.0 - beta_one ** step_count
    correct_two = 1.0 - beta_two ** step_count
    update = new_moment_one / correct_one / (jnp.sqrt(new_moment_two / correct_two) + adam_eps)
    new_master = master - adam_lr * (update + decay_rate * master)
    rollout = by_expert(new_master.astype(jnp.bfloat16))
    flat_x = dec_tokens.reshape(STEPS * DEC_ROWS, D)
    flat_ids = dec_routes.reshape(STEPS * DEC_ROWS)
    dec_total = STEPS * DCAP * N_GROUP

    def add_expert(carry, expert):
        chosen = flat_ids == expert
        index = jnp.nonzero(chosen, size=dec_total, fill_value=0)[0]
        valid = jnp.arange(dec_total) < jnp.sum(chosen.astype(jnp.int32))
        x_rows = flat_x[index]
        w_exp = lax.dynamic_index_in_dim(rollout, expert, 0, keepdims=False)
        dec_gate = jnp.dot(x_rows, w_exp[:, :D].T, preferred_element_type=jnp.float32)
        dec_up = jnp.dot(x_rows, w_exp[:, D:2 * D].T, preferred_element_type=jnp.float32)
        silu_val, unused_grad = silu_parts(dec_gate)
        dec_act = (silu_val * dec_up).astype(jnp.bfloat16)
        expert_out = jnp.dot(dec_act, w_exp[:, 2 * D:], preferred_element_type=jnp.float32).astype(jnp.bfloat16)
        expert_out = lax.optimization_barrier(expert_out).astype(jnp.float32)
        carry = carry.at[index].add(jnp.where(valid[:, None], expert_out, jnp.zeros((), jnp.float32)))
        return (carry, None)
    start_rows = jnp.zeros((STEPS * DEC_ROWS, D), jnp.float32)
    combined, unused_out = lax.scan(add_expert, start_rows, jnp.arange(EXPERTS, dtype=jnp.int32))
    dec_out = (dec_scale.reshape(STEPS * DEC_ROWS, 1) * combined).astype(jnp.bfloat16).reshape(STEPS, DEC_ROWS, D)
    return (new_master, new_moment_one, new_moment_two, dec_out)
```

```python
import functools

import jax
import jax.numpy as jnp
from jax import lax
from jax.experimental import pallas as pl
from jax.experimental.pallas import tpu as pltpu
from jax.sharding import PartitionSpec as P

EXPERTS = 8
CAP = 24
DCAP = 4


adam_lr = 0.001
beta_one = 0.9
beta_two = 0.95
adam_eps = 1e-08
decay_rate = 0.1
step_count = 100.0


def shifted(value, axis, by):
    count = lax.axis_size(axis)
    return lax.ppermute(value, axis, [(i, (i + by) % count) for i in range(count)])


def silu_parts(values):
    sig = jax.nn.sigmoid(values)
    return (values * sig, sig * (1.0 + values * (1.0 - sig)))


def rank_within(route_ids, experts, axis_dim):
    onehot = (route_ids[..., None] == jnp.arange(experts, dtype=jnp.int32)).astype(jnp.int32)
    running = jnp.cumsum(onehot, axis=axis_dim) - 1
    return jnp.sum(running * onehot, axis=-1)


def send_rows(value):
    return lax.all_to_all(value, "group", split_axis=1, concat_axis=1, tiled=True)


def from_peers(value, experts, split, axis_dim):
    parts = [value]
    for offset in range(1, split):
        parts.append(shifted(value, "group", offset * experts))
    return jnp.concatenate(parts, axis_dim)


def contract_rows(left, right):
    return lax.dot_general(
        left, right, (((1,), (1,)), ((), ())), preferred_element_type=jnp.float32
    )


def shards(
    tokens,
    routes,
    gate_scale,
    cotangent,
    master,
    moment_one,
    moment_two,
    dec_tokens,
    dec_routes,
    dec_scale,
):
    groups = lax.axis_size("group")
    replicas = lax.axis_size("dp")
    experts = EXPERTS
    split = groups // experts
    width = tokens.shape[1]
    capacity = CAP
    route_ids = routes[:, 0]
    slot_index = rank_within(route_ids, experts, 0)
    scaled = (gate_scale * cotangent.astype(jnp.float32)).astype(jnp.bfloat16)
    position = route_ids * capacity + slot_index
    select = (jnp.arange(experts * capacity, dtype=jnp.int32)[:, None] == position[None, :]).astype(
        jnp.bfloat16
    )
    packed = jnp.stack(
        [
            jnp.dot(select, tokens, preferred_element_type=jnp.float32),
            jnp.dot(select, scaled, preferred_element_type=jnp.float32),
        ],
        0,
    ).astype(jnp.bfloat16)
    packed = packed.reshape(2, 1, experts * capacity, width)
    tiled = jnp.broadcast_to(packed, (2, split, experts * capacity, width)).reshape(
        2, groups, capacity, width
    )
    arrived = send_rows(tiled)
    row_data = arrived.reshape(2, groups * capacity, width)
    x_rows = row_data[0]
    d_rows = row_data[1]
    master_rows = master[0]
    slice_w = lax.all_gather(master_rows.astype(jnp.bfloat16), "dp", axis=0, tiled=True)
    gate_pre = contract_rows(x_rows, slice_w[:, :width])
    up_pre = contract_rows(x_rows, slice_w[:, width : 2 * width])
    back_pre = contract_rows(d_rows, slice_w[:, 2 * width :])
    silu_val, silu_grad = silu_parts(gate_pre)
    activated = (silu_val * up_pre).astype(jnp.bfloat16)
    grad_up = (back_pre * silu_val).astype(jnp.bfloat16)
    grad_gate = (back_pre * up_pre * silu_grad).astype(jnp.bfloat16)
    pieces = []
    for source, operand in ((grad_gate, x_rows), (grad_up, x_rows), (activated, d_rows)):
        pieces.append(
            lax.dot_general(
                source, operand, (((0,), (0,)), ((), ())), preferred_element_type=jnp.float32
            )
        )
    grads = lax.psum_scatter(jnp.concatenate(pieces, 1), "dp", scatter_dimension=0, tiled=True)
    moment_new = beta_one * moment_one[0] + (1.0 - beta_one) * grads
    second_new = beta_two * moment_two[0] + (1.0 - beta_two) * grads * grads
    correct_one = 1.0 - beta_one**step_count
    correct_two = 1.0 - beta_two**step_count
    update = moment_new / correct_one / (jnp.sqrt(second_new / correct_two) + adam_eps)
    master_new = master_rows - adam_lr * (update + decay_rate * master_rows)
    rollout = from_peers(master_new.astype(jnp.bfloat16), experts, split, 0)
    per_peer = DCAP // split
    out_width = width // replicas
    own_index = lax.axis_index("group")
    outputs = []
    for step_index in range(dec_tokens.shape[0]):
        inputs = dec_tokens[step_index : step_index + 1]
        steps_here = inputs.shape[0]
        ids_now = dec_routes[step_index : step_index + 1][..., 0]
        slot_now = rank_within(ids_now, experts, 1)
        block_now = (slot_now // per_peer + own_index) % split
        decode_position = (
            block_now * (experts * per_peer) + ids_now * per_peer + slot_now % per_peer
        )
        decode_select = (
            jnp.arange(groups * per_peer, dtype=jnp.int32)[None, :, None]
            == decode_position[:, None, :]
        ).astype(jnp.bfloat16)
        decode_packed = jnp.einsum(
            "spr,srd->spd", decode_select, inputs, preferred_element_type=jnp.float32
        ).astype(jnp.bfloat16)
        decode_arrived = send_rows(decode_packed.reshape(steps_here, groups, per_peer, width))
        dec_rows = decode_arrived.reshape(steps_here * groups * per_peer, width)
        dec_gate = contract_rows(dec_rows, rollout[:, :width])
        dec_up = contract_rows(dec_rows, rollout[:, width : 2 * width])
        dec_silu, unused_grad = silu_parts(dec_gate)
        dec_act = (dec_silu * dec_up).astype(jnp.bfloat16)
        down_columns = lax.dynamic_slice_in_dim(
            rollout, 2 * width, out_width * lax.axis_size("dp"), 1
        )
        summed = lax.psum_scatter(
            lax.dot_general(
                down_columns, dec_act, (((0,), (1,)), ((), ())), preferred_element_type=jnp.float32
            ),
            "dp",
            scatter_dimension=0,
            tiled=True,
        )
        expert_out = summed.T.astype(jnp.bfloat16).reshape(steps_here, groups, per_peer, out_width)
        returned = send_rows(expert_out).reshape(steps_here, groups * per_peer, out_width)
        picked = jnp.einsum(
            "spr,spd->srd", decode_select, returned, preferred_element_type=jnp.float32
        )
        outputs.append((dec_scale[step_index : step_index + 1] * picked).astype(jnp.bfloat16))
    dec_out = jnp.concatenate(outputs, 0)
    return (master_new[None], moment_new[None], second_new[None], dec_out)


MESH = pl.DeviceIdType.MESH
CONTRACT_MINOR = (((1,), (1,)), ((), ()))
CONTRACT_MAJOR = (((0,), (0,)), ((), ()))


def pick_tile(width):
    return 512 if width % 512 == 0 else 128


def greet_peers(own_group, own_dp, groups):
    barrier = pltpu.get_barrier_semaphore()
    for step in range(1, groups):
        pl.semaphore_signal(
            barrier,
            inc=1,
            device_id={"group": lax.rem(own_group + step, groups), "dp": own_dp},
            device_id_type=MESH,
        )
    pl.semaphore_signal(
        barrier, inc=1, device_id={"group": own_group, "dp": 1 - own_dp}, device_id_type=MESH
    )
    pl.semaphore_wait(barrier, groups)


def learner_kernel(
    groups,
    tok,
    cot,
    gate_scale,
    sel,
    dtok,
    dsel,
    master,
    grads,
    drows_out,
    packed,
    rows,
    dpacked,
    drows,
    weights,
    pre,
    left,
    near_send,
    near_recv,
    half_send,
    half_recv,
    side_send,
    side_recv,
    dnear_send,
    dnear_recv,
    dhalf_send,
    dhalf_recv,
    dside_send,
    dside_recv,
    out_sem,
):
    group = lax.axis_index("group")
    dp = lax.axis_index("dp")
    half = group // EXPERTS
    expert = lax.rem(group, EXPERTS)
    width = tok.shape[1]
    hidden = weights.shape[0]
    tile = pick_tile(width)
    block = 2 * CAP
    chunk = EXPERTS * block

    def remote(src, dst, send, recv, to_group, to_dp):
        return pltpu.make_async_remote_copy(
            src_ref=src,
            dst_ref=dst,
            send_sem=send,
            recv_sem=recv,
            device_id={"group": to_group, "dp": to_dp},
            device_id_type=MESH,
        )

    @pl.loop(0, width // tile)
    def _(index):
        columns = pl.ds(pl.multiple_of(index * tile, tile), tile)
        scaled = (gate_scale[...] * cot[:, columns].astype(jnp.float32)).astype(jnp.bfloat16)
        both = jnp.concatenate([tok[:, columns], scaled], 0)
        picked = jnp.dot(sel[...], both, preferred_element_type=jnp.float32).astype(jnp.bfloat16)
        packed[:, :, columns] = picked.reshape(EXPERTS, block, tile)
        picked = jnp.dot(dsel[...], dtok[:, columns], preferred_element_type=jnp.float32)
        dpacked[:, :, columns] = picked.astype(jnp.bfloat16).reshape(EXPERTS, -1, tile)

    greet_peers(group, dp, groups)

    near = [None] + [
        remote(
            packed.at[lax.rem(expert + step, EXPERTS)],
            rows.at[0, 0, step],
            near_send.at[step],
            near_recv.at[step],
            half * EXPERTS + lax.rem(expert + step, EXPERTS),
            dp,
        )
        for step in range(1, EXPERTS)
    ]
    other_group = (1 - half) * EXPERTS + expert
    across = []
    beside = []
    for step in range(EXPERTS):
        source = packed.at[expert] if step == 0 else rows.at[0, 0, step]
        across.append(
            remote(
                source,
                rows.at[0, 1, step],
                half_send.at[step],
                half_recv.at[step],
                other_group,
                dp,
            )
        )
        beside.append(
            remote(
                source,
                rows.at[1, 0, step],
                side_send.at[0, step],
                side_recv.at[0, step],
                group,
                1 - dp,
            )
        )
    further = [
        remote(
            rows.at[0, 1, step],
            rows.at[1, 1, step],
            side_send.at[1, step],
            side_recv.at[1, step],
            group,
            1 - dp,
        )
        for step in range(EXPERTS)
    ]
    dnear = [None] + [
        remote(
            dpacked.at[lax.rem(expert + step, EXPERTS)],
            drows.at[0, step],
            dnear_send.at[step],
            dnear_recv.at[step],
            half * EXPERTS + lax.rem(expert + step, EXPERTS),
            dp,
        )
        for step in range(1, EXPERTS)
    ]
    dacross = []
    dbeside = []
    for index in range(EXPERTS // 2):
        step = 2 * index + dp
        dacross.append(
            remote(
                dpacked.at[lax.rem(expert + step, EXPERTS)],
                drows.at[1, step],
                dhalf_send.at[index],
                dhalf_recv.at[index],
                (1 - half) * EXPERTS + lax.rem(expert + step, EXPERTS),
                dp,
            )
        )
        dbeside.append(
            remote(
                drows.at[1, step],
                drows.at[1, step],
                dside_send.at[index],
                dside_recv.at[index],
                group,
                1 - dp,
            )
        )

    across[0].start()
    beside[0].start()
    for step in range(1, EXPERTS):
        near[step].start()
    rows[0, 0, 0] = packed[expert]
    drows[0, 0] = dpacked[expert]

    lines = min(16, hidden)

    def cast_body(source):
        begin = pl.multiple_of(pl.program_id(0) * lines, lines)
        weights[pl.ds(begin, lines), :] = source[...].astype(jnp.bfloat16)

    pltpu.emit_pipeline(
        cast_body,
        grid=(hidden // lines,),
        in_specs=[pl.BlockSpec((lines, 3 * width), lambda i: (i, 0))],
        out_specs=[],
    )(master)

    for step in range(1, EXPERTS):
        near[step].wait_recv()
        across[step].start()
        beside[step].start()

    def learn(side, far, first):
        own = rows.at[side, far]
        pre[...] = jnp.zeros_like(pre)

        @pl.loop(0, width // tile)
        def _(index):
            start = pl.multiple_of(index * tile, tile)
            operand = own[:, :, pl.ds(start, tile)].reshape(chunk, tile)
            for part in range(3):
                begin = pl.multiple_of(part * width + start, 128)
                pre[:, part * hidden : (part + 1) * hidden] += lax.dot_general(
                    operand,
                    weights[:, pl.ds(begin, tile)],
                    CONTRACT_MINOR,
                    preferred_element_type=jnp.float32,
                )

        parts = pre[...].reshape(EXPERTS, block, 3 * hidden)
        gate_pre = parts[:, :CAP, :hidden]
        up_pre = parts[:, :CAP, hidden : 2 * hidden]
        back_pre = parts[:, CAP:, 2 * hidden :]
        silu_val, silu_grad = silu_parts(gate_pre)
        zeros = jnp.zeros_like(gate_pre)
        top = jnp.concatenate([back_pre * up_pre * silu_grad, back_pre * silu_val, zeros], 2)
        bottom = jnp.concatenate([zeros, zeros, silu_val * up_pre], 2)
        left[...] = (
            jnp.concatenate([top, bottom], 1)
            .reshape(chunk, 3 * hidden)
            .T.astype(jnp.bfloat16)
        )

        @pl.loop(0, width // tile)
        def _(index):
            columns = pl.ds(pl.multiple_of(index * tile, tile), tile)
            operand = own[:, :, columns].reshape(chunk, tile)
            value = jnp.dot(left[...], operand, preferred_element_type=jnp.float32)
            if first:
                grads[:, columns] = value
            else:
                grads[:, columns] += value

    learn(0, 0, True)
    for step in range(EXPERTS):
        across[step].wait_recv()
        further[step].start()
        if step == EXPERTS - 3:
            for index in range(EXPERTS // 2):
                dacross[index].start()
            for other in range(1, EXPERTS):
                dnear[other].start()
    for step in range(EXPERTS):
        beside[step].wait_recv()
    learn(1, 0, False)
    for index in range(EXPERTS // 2):
        dacross[index].wait_recv()
        dbeside[index].start()
    learn(0, 1, False)
    for step in range(EXPERTS):
        further[step].wait_recv()
    learn(1, 1, False)
    for step in range(1, EXPERTS):
        dnear[step].wait_recv()
    for index in range(EXPERTS // 2):
        step = 2 * index + 1 - dp
        remote(
            drows.at[1, step],
            drows.at[1, step],
            dside_send.at[index],
            dside_recv.at[index],
            group,
            1 - dp,
        ).wait_recv()
    leave = pltpu.make_async_copy(drows, drows_out, out_sem)
    leave.start()
    leave.wait()
    for step in range(EXPERTS):
        across[step].wait_send()
        beside[step].wait_send()
        further[step].wait_send()
        if step:
            near[step].wait_send()
            dnear[step].wait_send()
    for index in range(EXPERTS // 2):
        dacross[index].wait_send()
        dbeside[index].wait_send()


def decode_kernel(
    groups,
    drows,
    roll,
    dsel,
    dscale,
    out,
    pre,
    own,
    side_out,
    side_in,
    back_out,
    back_in,
    side_send,
    side_recv,
    back_send,
    back_recv,
):
    group = lax.axis_index("group")
    dp = lax.axis_index("dp")
    half = group // EXPERTS
    expert = lax.rem(group, EXPERTS)
    hidden, wide = roll.shape
    width = wide // 3
    out_width = width // 2
    tile = pick_tile(width)
    slots = drows.shape[0] // (2 * EXPERTS)
    pieces = side_out.shape[0]
    per_piece = 2 * EXPERTS // pieces
    greet_peers(group, dp, groups)
    pre[...] = jnp.zeros_like(pre)

    @pl.loop(0, width // tile)
    def _(index):
        start = pl.multiple_of(index * tile, tile)
        operand = drows[:, pl.ds(start, tile)]
        for part in range(2):
            begin = pl.multiple_of(part * width + start, 128)
            pre[:, part * hidden : (part + 1) * hidden] += lax.dot_general(
                operand,
                roll[:, pl.ds(begin, tile)],
                CONTRACT_MINOR,
                preferred_element_type=jnp.float32,
            )

    dec_silu, unused_grad = silu_parts(pre[:, :hidden])
    act = (dec_silu * pre[:, hidden:]).astype(jnp.bfloat16)
    strip = 256 if out_width % 256 == 0 else 128
    for index in range(out_width // strip):
        begin = pl.multiple_of(2 * width + (1 - dp) * out_width + index * strip, 128)
        value = jnp.dot(act, roll[:, pl.ds(begin, strip)], preferred_element_type=jnp.float32)
        side_out[:, :, index * strip : (index + 1) * strip] = value.astype(jnp.bfloat16).reshape(
            pieces, -1, strip
        )
    order = list(range(pieces // 2, pieces)) + list(range(pieces // 2))
    side = [
        pltpu.make_async_remote_copy(
            src_ref=side_out.at[piece],
            dst_ref=side_in.at[piece],
            send_sem=side_send.at[piece],
            recv_sem=side_recv.at[piece],
            device_id={"group": group, "dp": 1 - dp},
            device_id_type=MESH,
        )
        for piece in range(pieces)
    ]
    for piece in order:
        side[piece].start()
    for index in range(out_width // strip):
        begin = pl.multiple_of(2 * width + dp * out_width + index * strip, 128)
        value = jnp.dot(act, roll[:, pl.ds(begin, strip)], preferred_element_type=jnp.float32)
        own[:, :, index * strip : (index + 1) * strip] = value.reshape(pieces, -1, strip)
    back = {}
    for piece in order:
        side[piece].wait_recv()
        total = (own[piece] + side_in[piece].astype(jnp.float32)).astype(jnp.bfloat16)
        total = total.reshape(per_piece, slots, out_width)
        for place in range(per_piece):
            far, step = divmod(piece * per_piece + place, EXPERTS)
            if far == 0 and step == 0:
                back_in[0, 0] = total[place]
                continue
            back_out[far, step] = total[place]
            to_half = 1 - half if far else half
            back[far, step] = pltpu.make_async_remote_copy(
                src_ref=back_out.at[far, step],
                dst_ref=back_in.at[far, step],
                send_sem=back_send.at[far, step],
                recv_sem=back_recv.at[far, step],
                device_id={
                    "group": to_half * EXPERTS + lax.rem(expert + EXPERTS - step, EXPERTS),
                    "dp": dp,
                },
                device_id_type=MESH,
            )
            back[far, step].start()
    for copy in back.values():
        copy.wait_recv()
    total = (back_in[0].astype(jnp.float32) + back_in[1].astype(jnp.float32)).astype(jnp.bfloat16)
    total = total.reshape(EXPERTS * slots, out_width)
    picked = lax.dot_general(
        dsel[...], total, CONTRACT_MAJOR, preferred_element_type=jnp.float32
    )
    out[...] = (dscale[...] * picked).astype(jnp.bfloat16)
    for copy in back.values():
        copy.wait_send()
    for copy in side:
        copy.wait_send()


def moved_rows(
    tokens,
    routes,
    gate_scale,
    cotangent,
    master,
    moment_one,
    moment_two,
    dec_tokens,
    dec_routes,
    dec_scale,
):
    groups = lax.axis_size("group")
    width = tokens.shape[1]
    hidden = master.shape[1]
    steps, dec_here = dec_tokens.shape[:2]
    slots = steps * DCAP
    own_expert = lax.rem(lax.axis_index("group"), EXPERTS)
    route_ids = routes[:, 0]
    position = route_ids * (2 * CAP) + rank_within(route_ids, EXPERTS, 0)
    position = jnp.concatenate([position, position + CAP])
    sel = (
        jnp.arange(EXPERTS * 2 * CAP, dtype=jnp.int32)[:, None] == position[None, :]
    ).astype(jnp.bfloat16)
    dec_ids = dec_routes[..., 0]
    within = rank_within(dec_ids, EXPERTS, 1) + DCAP * jnp.arange(steps, dtype=jnp.int32)[:, None]
    dec_place = jnp.arange(EXPERTS * slots, dtype=jnp.int32)[:, None]
    dsel = (dec_place == (dec_ids * slots + within).reshape(1, -1)).astype(jnp.bfloat16)
    turned = lax.rem(dec_ids + EXPERTS - own_expert, EXPERTS)
    back_sel = (dec_place == (turned * slots + within).reshape(1, -1)).astype(jnp.bfloat16)

    master_rows = master[0]
    vmem = pl.BlockSpec(memory_space=pltpu.VMEM)
    anywhere = pl.BlockSpec(memory_space=pl.ANY)
    dma = pltpu.SemaphoreType.DMA
    rows_all = 2 * 2 * EXPERTS * 2 * CAP
    grads, drows = pl.pallas_call(
        functools.partial(learner_kernel, groups),
        out_shape=(
            jax.ShapeDtypeStruct((3 * hidden, width), jnp.float32),
            jax.ShapeDtypeStruct((2, EXPERTS, slots, width), jnp.bfloat16),
        ),
        in_specs=[vmem] * 6 + [anywhere],
        out_specs=(vmem, anywhere),
        scratch_shapes=[
            pltpu.VMEM((EXPERTS, 2 * CAP, width), jnp.bfloat16),
            pltpu.VMEM((2, 2, EXPERTS, 2 * CAP, width), jnp.bfloat16),
            pltpu.VMEM((EXPERTS, slots, width), jnp.bfloat16),
            pltpu.VMEM((2, EXPERTS, slots, width), jnp.bfloat16),
            pltpu.VMEM((hidden, 3 * width), jnp.bfloat16),
            pltpu.VMEM((EXPERTS * 2 * CAP, 3 * hidden), jnp.float32),
            pltpu.VMEM((3 * hidden, EXPERTS * 2 * CAP), jnp.bfloat16),
            dma((EXPERTS,)),
            dma((EXPERTS,)),
            dma((EXPERTS,)),
            dma((EXPERTS,)),
            dma((2, EXPERTS)),
            dma((2, EXPERTS)),
            dma((EXPERTS,)),
            dma((EXPERTS,)),
            dma((EXPERTS // 2,)),
            dma((EXPERTS // 2,)),
            dma((EXPERTS // 2,)),
            dma((EXPERTS // 2,)),
            dma(()),
        ],
        compiler_params=pltpu.CompilerParams(
            collective_id=0, has_side_effects=True, vmem_limit_bytes=56 * 2**20
        ),
        cost_estimate=pl.CostEstimate(
            flops=12 * rows_all * hidden * width,
            bytes_accessed=24 * hidden * width,
            transcendentals=rows_all * hidden,
        ),
        name="learner",
    )(
        tokens,
        cotangent,
        gate_scale,
        sel,
        dec_tokens.reshape(steps * dec_here, width),
        dsel,
        master_rows,
    )
    grads = jnp.concatenate(
        [grads[part * hidden : (part + 1) * hidden] for part in range(3)], 1
    )
    moment_new = beta_one * moment_one[0] + (1.0 - beta_one) * grads
    second_new = beta_two * moment_two[0] + (1.0 - beta_two) * grads * grads
    correct_one = 1.0 - beta_one**step_count
    correct_two = 1.0 - beta_two**step_count
    update = moment_new / correct_one / (jnp.sqrt(second_new / correct_two) + adam_eps)
    master_new = master_rows - adam_lr * (update + decay_rate * master_rows)
    rollout = master_new.astype(jnp.bfloat16)
    out_width = width // 2
    rows_dec = 2 * EXPERTS * slots
    pieces = 4
    dec_out = pl.pallas_call(
        functools.partial(decode_kernel, groups),
        out_shape=jax.ShapeDtypeStruct((steps * dec_here, out_width), jnp.bfloat16),
        in_specs=[vmem] * 4,
        out_specs=vmem,
        scratch_shapes=[
            pltpu.VMEM((rows_dec, 2 * hidden), jnp.float32),
            pltpu.VMEM((pieces, rows_dec // pieces, out_width), jnp.float32),
            pltpu.VMEM((pieces, rows_dec // pieces, out_width), jnp.bfloat16),
            pltpu.VMEM((pieces, rows_dec // pieces, out_width), jnp.bfloat16),
            pltpu.VMEM((2, EXPERTS, slots, out_width), jnp.bfloat16),
            pltpu.VMEM((2, EXPERTS, slots, out_width), jnp.bfloat16),
            dma((pieces,)),
            dma((pieces,)),
            dma((2, EXPERTS)),
            dma((2, EXPERTS)),
        ],
        compiler_params=pltpu.CompilerParams(
            collective_id=1, has_side_effects=True, vmem_limit_bytes=40 * 2**20
        ),
        cost_estimate=pl.CostEstimate(
            flops=6 * rows_dec * hidden * width,
            bytes_accessed=6 * hidden * width,
            transcendentals=rows_dec * hidden,
        ),
        name="decode",
    )(
        drows.reshape(rows_dec, width),
        rollout,
        back_sel,
        dec_scale.reshape(steps * dec_here, 1),
    )
    return (
        master_new[None],
        moment_new[None],
        second_new[None],
        dec_out.reshape(steps, dec_here, out_width),
    )


def solution(mesh):
    in_specs = (
        P(("group", "dp"), None),
        P(("group", "dp"), None),
        P(("group", "dp"), None),
        P(("group", "dp"), None),
        P("group", "dp", None),
        P("group", "dp", None),
        P("group", "dp", None),
        P(None, "group", None),
        P(None, "group", None),
        P(None, "group", None),
    )
    out_specs = (
        P("group", "dp", None),
        P("group", "dp", None),
        P("group", "dp", None),
        P(None, "group", "dp"),
    )
    in_place = mesh.shape["group"] == 2 * EXPERTS and mesh.shape["dp"] == 2
    body = moved_rows if in_place else shards
    return jax.shard_map(body, mesh=mesh, in_specs=in_specs, out_specs=out_specs, check_vma=False)
```

```python
import functools

import jax
import jax.numpy as jnp
from jax import lax
from jax.experimental import pallas as pl
from jax.experimental.pallas import tpu as pltpu
from jax.sharding import PartitionSpec as P

EXPERTS = 8
CAP = 24
DCAP = 4


adam_lr = 0.001
beta_one = 0.9
beta_two = 0.95
adam_eps = 1e-08
decay_rate = 0.1
step_count = 100.0


def shifted(value, axis, by):
    count = lax.axis_size(axis)
    return lax.ppermute(value, axis, [(i, (i + by) % count) for i in range(count)])


def silu_parts(values):
    sig = jax.nn.sigmoid(values)
    return (values * sig, sig * (1.0 + values * (1.0 - sig)))


def rank_within(route_ids, experts, axis_dim):
    onehot = (route_ids[..., None] == jnp.arange(experts, dtype=jnp.int32)).astype(jnp.int32)
    running = jnp.cumsum(onehot, axis=axis_dim) - 1
    return jnp.sum(running * onehot, axis=-1)


def send_rows(value):
    return lax.all_to_all(value, "group", split_axis=1, concat_axis=1, tiled=True)


def from_peers(value, experts, split, axis_dim):
    parts = [value]
    for offset in range(1, split):
        parts.append(shifted(value, "group", offset * experts))
    return jnp.concatenate(parts, axis_dim)


def contract_rows(left, right):
    return lax.dot_general(
        left, right, (((1,), (1,)), ((), ())), preferred_element_type=jnp.float32
    )


def shards(
    tokens,
    routes,
    gate_scale,
    cotangent,
    master,
    moment_one,
    moment_two,
    dec_tokens,
    dec_routes,
    dec_scale,
):
    groups = lax.axis_size("group")
    replicas = lax.axis_size("dp")
    experts = EXPERTS
    split = groups // experts
    width = tokens.shape[1]
    capacity = CAP
    route_ids = routes[:, 0]
    slot_index = rank_within(route_ids, experts, 0)
    scaled = (gate_scale * cotangent.astype(jnp.float32)).astype(jnp.bfloat16)
    position = route_ids * capacity + slot_index
    select = (jnp.arange(experts * capacity, dtype=jnp.int32)[:, None] == position[None, :]).astype(
        jnp.bfloat16
    )
    packed = jnp.stack(
        [
            jnp.dot(select, tokens, preferred_element_type=jnp.float32),
            jnp.dot(select, scaled, preferred_element_type=jnp.float32),
        ],
        0,
    ).astype(jnp.bfloat16)
    packed = packed.reshape(2, 1, experts * capacity, width)
    tiled = jnp.broadcast_to(packed, (2, split, experts * capacity, width)).reshape(
        2, groups, capacity, width
    )
    arrived = send_rows(tiled)
    row_data = arrived.reshape(2, groups * capacity, width)
    x_rows = row_data[0]
    d_rows = row_data[1]
    master_rows = master[0]
    slice_w = lax.all_gather(master_rows.astype(jnp.bfloat16), "dp", axis=0, tiled=True)
    gate_pre = contract_rows(x_rows, slice_w[:, :width])
    up_pre = contract_rows(x_rows, slice_w[:, width : 2 * width])
    back_pre = contract_rows(d_rows, slice_w[:, 2 * width :])
    silu_val, silu_grad = silu_parts(gate_pre)
    activated = (silu_val * up_pre).astype(jnp.bfloat16)
    grad_up = (back_pre * silu_val).astype(jnp.bfloat16)
    grad_gate = (back_pre * up_pre * silu_grad).astype(jnp.bfloat16)
    pieces = []
    for source, operand in ((grad_gate, x_rows), (grad_up, x_rows), (activated, d_rows)):
        pieces.append(
            lax.dot_general(
                source, operand, (((0,), (0,)), ((), ())), preferred_element_type=jnp.float32
            )
        )
    grads = lax.psum_scatter(jnp.concatenate(pieces, 1), "dp", scatter_dimension=0, tiled=True)
    moment_new = beta_one * moment_one[0] + (1.0 - beta_one) * grads
    second_new = beta_two * moment_two[0] + (1.0 - beta_two) * grads * grads
    correct_one = 1.0 - beta_one**step_count
    correct_two = 1.0 - beta_two**step_count
    update = moment_new / correct_one / (jnp.sqrt(second_new / correct_two) + adam_eps)
    master_new = master_rows - adam_lr * (update + decay_rate * master_rows)
    rollout = from_peers(master_new.astype(jnp.bfloat16), experts, split, 0)
    per_peer = DCAP // split
    out_width = width // replicas
    own_index = lax.axis_index("group")
    outputs = []
    for step_index in range(dec_tokens.shape[0]):
        inputs = dec_tokens[step_index : step_index + 1]
        steps_here = inputs.shape[0]
        ids_now = dec_routes[step_index : step_index + 1][..., 0]
        slot_now = rank_within(ids_now, experts, 1)
        block_now = (slot_now // per_peer + own_index) % split
        decode_position = (
            block_now * (experts * per_peer) + ids_now * per_peer + slot_now % per_peer
        )
        decode_select = (
            jnp.arange(groups * per_peer, dtype=jnp.int32)[None, :, None]
            == decode_position[:, None, :]
        ).astype(jnp.bfloat16)
        decode_packed = jnp.einsum(
            "spr,srd->spd", decode_select, inputs, preferred_element_type=jnp.float32
        ).astype(jnp.bfloat16)
        decode_arrived = send_rows(decode_packed.reshape(steps_here, groups, per_peer, width))
        dec_rows = decode_arrived.reshape(steps_here * groups * per_peer, width)
        dec_gate = contract_rows(dec_rows, rollout[:, :width])
        dec_up = contract_rows(dec_rows, rollout[:, width : 2 * width])
        dec_silu, unused_grad = silu_parts(dec_gate)
        dec_act = (dec_silu * dec_up).astype(jnp.bfloat16)
        down_columns = lax.dynamic_slice_in_dim(
            rollout, 2 * width, out_width * lax.axis_size("dp"), 1
        )
        summed = lax.psum_scatter(
            lax.dot_general(
                down_columns, dec_act, (((0,), (1,)), ((), ())), preferred_element_type=jnp.float32
            ),
            "dp",
            scatter_dimension=0,
            tiled=True,
        )
        expert_out = summed.T.astype(jnp.bfloat16).reshape(steps_here, groups, per_peer, out_width)
        returned = send_rows(expert_out).reshape(steps_here, groups * per_peer, out_width)
        picked = jnp.einsum(
            "spr,spd->srd", decode_select, returned, preferred_element_type=jnp.float32
        )
        outputs.append((dec_scale[step_index : step_index + 1] * picked).astype(jnp.bfloat16))
    dec_out = jnp.concatenate(outputs, 0)
    return (master_new[None], moment_new[None], second_new[None], dec_out)


MESH = pl.DeviceIdType.MESH
CONTRACT_MINOR = (((1,), (1,)), ((), ()))
CONTRACT_MAJOR = (((0,), (0,)), ((), ()))


def pick_tile(width):
    return 512 if width % 512 == 0 else 128


def count_before(ids, group_of):
    count = ids.shape[1]
    lines = lax.broadcasted_iota(jnp.int32, (16, count), 0)
    onehot = (lines == ids).astype(jnp.float32)
    earlier = lax.broadcasted_iota(jnp.int32, (count, count), 0)
    later = lax.broadcasted_iota(jnp.int32, (count, count), 1)
    before = (earlier < later) & (earlier // group_of == later // group_of)
    running = jnp.dot(
        onehot.astype(jnp.bfloat16),
        before.astype(jnp.float32).astype(jnp.bfloat16),
        preferred_element_type=jnp.float32,
    )
    return jnp.sum(running * onehot, axis=0, keepdims=True)


def as_column(line):
    count = line.shape[1]
    across = lax.broadcasted_iota(jnp.int32, (count, count), 0)
    along = lax.broadcasted_iota(jnp.int32, (count, count), 1)
    return jnp.sum(jnp.where(across == along, line, 0.0), axis=1, keepdims=True)


def one_hot_rows(count, place):
    lines = lax.broadcasted_iota(jnp.int32, (count, place.shape[1]), 0).astype(jnp.float32)
    return (lines == place).astype(jnp.float32).astype(jnp.bfloat16)


def decode_place(ids, step_rows, slots, turned):
    step_of = lax.broadcasted_iota(jnp.int32, ids.shape, 1) // step_rows
    within = (step_of * DCAP).astype(jnp.float32) + count_before(ids, step_rows)
    return (turned * slots).astype(jnp.float32) + within


def greet_peers(own_group, own_dp, groups):
    barrier = pltpu.get_barrier_semaphore()
    for step in range(1, groups):
        pl.semaphore_signal(
            barrier,
            inc=1,
            device_id={"group": lax.rem(own_group + step, groups), "dp": own_dp},
            device_id_type=MESH,
        )
    pl.semaphore_signal(
        barrier, inc=1, device_id={"group": own_group, "dp": 1 - own_dp}, device_id_type=MESH
    )
    pl.semaphore_wait(barrier, groups)


def learner_kernel(
    groups,
    step_rows,
    tok,
    cot,
    scale_line,
    routes,
    dtok,
    droutes,
    master,
    grads_out,
    drows_out,
    grads,
    gate_scale,
    sel,
    dsel,
    packed,
    rows,
    dpacked,
    drows,
    weights,
    pre,
    left,
    near_send,
    near_recv,
    half_send,
    half_recv,
    side_send,
    side_recv,
    dnear_send,
    dnear_recv,
    dhalf_send,
    dhalf_recv,
    dside_send,
    dside_recv,
    out_sem,
    grads_sem,
):
    group = lax.axis_index("group")
    dp = lax.axis_index("dp")
    half = group // EXPERTS
    expert = lax.rem(group, EXPERTS)
    width = tok.shape[1]
    hidden = weights.shape[0]
    tile = pick_tile(width)
    block = 2 * CAP
    chunk = EXPERTS * block

    def remote(src, dst, send, recv, to_group, to_dp):
        return pltpu.make_async_remote_copy(
            src_ref=src,
            dst_ref=dst,
            send_sem=send,
            recv_sem=recv,
            device_id={"group": to_group, "dp": to_dp},
            device_id_type=MESH,
        )

    gate_scale[...] = as_column(scale_line[...])
    ids = routes[...]
    place = (ids * block).astype(jnp.float32) + count_before(ids, ids.shape[1])
    sel[...] = one_hot_rows(chunk, jnp.concatenate([place, place + CAP], 1))
    slots = dpacked.shape[1]
    ids = droutes[...]
    dsel[...] = one_hot_rows(EXPERTS * slots, decode_place(ids, step_rows, slots, ids))

    @pl.loop(0, width // tile)
    def _(index):
        columns = pl.ds(pl.multiple_of(index * tile, tile), tile)
        scaled = (gate_scale[...] * cot[:, columns].astype(jnp.float32)).astype(jnp.bfloat16)
        both = jnp.concatenate([tok[:, columns], scaled], 0)
        picked = jnp.dot(sel[...], both, preferred_element_type=jnp.float32).astype(jnp.bfloat16)
        packed[:, :, columns] = picked.reshape(EXPERTS, block, tile)
        picked = jnp.dot(dsel[...], dtok[:, columns], preferred_element_type=jnp.float32)
        dpacked[:, :, columns] = picked.astype(jnp.bfloat16).reshape(EXPERTS, -1, tile)

    greet_peers(group, dp, groups)

    near = [None] + [
        remote(
            packed.at[lax.rem(expert + step, EXPERTS)],
            rows.at[0, 0, step],
            near_send.at[step],
            near_recv.at[step],
            half * EXPERTS + lax.rem(expert + step, EXPERTS),
            dp,
        )
        for step in range(1, EXPERTS)
    ]
    other_group = (1 - half) * EXPERTS + expert
    across = []
    beside = []
    for step in range(EXPERTS):
        source = packed.at[expert] if step == 0 else rows.at[0, 0, step]
        across.append(
            remote(
                source,
                rows.at[0, 1, step],
                half_send.at[step],
                half_recv.at[step],
                other_group,
                dp,
            )
        )
        beside.append(
            remote(
                source,
                rows.at[1, 0, step],
                side_send.at[0, step],
                side_recv.at[0, step],
                group,
                1 - dp,
            )
        )
    further = [
        remote(
            rows.at[0, 1, step],
            rows.at[1, 1, step],
            side_send.at[1, step],
            side_recv.at[1, step],
            group,
            1 - dp,
        )
        for step in range(EXPERTS)
    ]
    dnear = [None] + [
        remote(
            dpacked.at[lax.rem(expert + step, EXPERTS)],
            drows.at[0, step],
            dnear_send.at[step],
            dnear_recv.at[step],
            half * EXPERTS + lax.rem(expert + step, EXPERTS),
            dp,
        )
        for step in range(1, EXPERTS)
    ]
    dacross = []
    dbeside = []
    for index in range(EXPERTS // 2):
        step = 2 * index + dp
        dacross.append(
            remote(
                dpacked.at[lax.rem(expert + step, EXPERTS)],
                drows.at[1, step],
                dhalf_send.at[index],
                dhalf_recv.at[index],
                (1 - half) * EXPERTS + lax.rem(expert + step, EXPERTS),
                dp,
            )
        )
        dbeside.append(
            remote(
                drows.at[1, step],
                drows.at[1, step],
                dside_send.at[index],
                dside_recv.at[index],
                group,
                1 - dp,
            )
        )

    across[0].start()
    beside[0].start()
    for step in range(1, EXPERTS):
        near[step].start()
    rows[0, 0, 0] = packed[expert]
    drows[0, 0] = dpacked[expert]

    lines = min(16, hidden)

    def cast_body(source):
        begin = pl.multiple_of(pl.program_id(0) * lines, lines)
        weights[pl.ds(begin, lines), :] = source[...].astype(jnp.bfloat16)

    pltpu.emit_pipeline(
        cast_body,
        grid=(hidden // lines,),
        in_specs=[pl.BlockSpec((lines, 3 * width), lambda i: (i, 0))],
        out_specs=[],
    )(master)

    for step in range(1, EXPERTS):
        near[step].wait_recv()
        across[step].start()
        beside[step].start()

    def learn(side, far, begin_step, steps, first=False, last=False):
        own = rows.at[side, far, pl.ds(begin_step, steps)]
        height = steps * block
        pre[:height] = jnp.zeros((height, 3 * hidden), jnp.float32)

        @pl.loop(0, width // tile)
        def _(index):
            start = pl.multiple_of(index * tile, tile)
            operand = own[:, :, pl.ds(start, tile)].reshape(height, tile)
            for part in range(3):
                begin = pl.multiple_of(part * width + start, 128)
                pre[:height, part * hidden : (part + 1) * hidden] += lax.dot_general(
                    operand,
                    weights[:, pl.ds(begin, tile)],
                    CONTRACT_MINOR,
                    preferred_element_type=jnp.float32,
                )

        parts = pre[:height].reshape(steps, block, 3 * hidden)
        gate_pre = parts[:, :CAP, :hidden]
        up_pre = parts[:, :CAP, hidden : 2 * hidden]
        back_pre = parts[:, CAP:, 2 * hidden :]
        silu_val, silu_grad = silu_parts(gate_pre)
        zeros = jnp.zeros_like(gate_pre)
        top = jnp.concatenate([back_pre * up_pre * silu_grad, back_pre * silu_val, zeros], 2)
        bottom = jnp.concatenate([zeros, zeros, silu_val * up_pre], 2)
        left[:, :height] = (
            jnp.concatenate([top, bottom], 1)
            .reshape(height, 3 * hidden)
            .T.astype(jnp.bfloat16)
        )

        @pl.loop(0, width // tile)
        def _(index):
            columns = pl.ds(pl.multiple_of(index * tile, tile), tile)
            operand = own[:, :, columns].reshape(height, tile)
            value = jnp.dot(left[:, :height], operand, preferred_element_type=jnp.float32)
            if first:
                grads[:, columns] = value
            else:
                grads[:, columns] += value
            if last:
                pltpu.make_async_copy(
                    grads.at[:, columns], grads_out.at[:, columns], grads_sem.at[index]
                ).start()

    learn(0, 0, 0, EXPERTS, first=True)
    for step in range(EXPERTS):
        across[step].wait_recv()
        further[step].start()
    for index in range(EXPERTS // 2):
        dacross[index].start()
    for step in range(1, EXPERTS):
        dnear[step].start()
    for step in range(EXPERTS):
        beside[step].wait_recv()
    learn(1, 0, 0, EXPERTS)
    learn(0, 1, 0, EXPERTS)
    for index in range(EXPERTS // 2):
        dacross[index].wait_recv()
        dbeside[index].start()
    for step in range(EXPERTS // 2):
        further[step].wait_recv()
    learn(1, 1, 0, EXPERTS // 2)
    for step in range(EXPERTS // 2, EXPERTS):
        further[step].wait_recv()
    learn(1, 1, EXPERTS // 2, EXPERTS // 2, last=True)
    for step in range(1, EXPERTS):
        dnear[step].wait_recv()
    for index in range(EXPERTS // 2):
        step = 2 * index + 1 - dp
        remote(
            drows.at[1, step],
            drows.at[1, step],
            dside_send.at[index],
            dside_recv.at[index],
            group,
            1 - dp,
        ).wait_recv()
    leave = pltpu.make_async_copy(drows, drows_out, out_sem)
    leave.start()

    @pl.loop(0, width // tile)
    def _(index):
        columns = pl.ds(pl.multiple_of(index * tile, tile), tile)
        pltpu.make_async_copy(
            grads.at[:, columns], grads_out.at[:, columns], grads_sem.at[index]
        ).wait()

    leave.wait()
    for step in range(EXPERTS):
        across[step].wait_send()
        beside[step].wait_send()
        further[step].wait_send()
        if step:
            near[step].wait_send()
            dnear[step].wait_send()
    for index in range(EXPERTS // 2):
        dacross[index].wait_send()
        dbeside[index].wait_send()


def decode_kernel(
    groups,
    step_rows,
    drows,
    roll,
    droutes,
    dscale,
    out,
    pre,
    own,
    side_out,
    side_in,
    back_out,
    back_in,
    side_send,
    side_recv,
    back_send,
    back_recv,
):
    group = lax.axis_index("group")
    dp = lax.axis_index("dp")
    half = group // EXPERTS
    expert = lax.rem(group, EXPERTS)
    hidden, wide = roll.shape
    width = wide // 3
    out_width = width // 2
    tile = pick_tile(width)
    slots = drows.shape[0] // (2 * EXPERTS)
    pieces = side_out.shape[0]
    per_piece = 2 * EXPERTS // pieces
    greet_peers(group, dp, groups)
    pre[...] = jnp.zeros_like(pre)

    @pl.loop(0, width // tile)
    def _(index):
        start = pl.multiple_of(index * tile, tile)
        operand = drows[:, pl.ds(start, tile)]
        for part in range(2):
            begin = pl.multiple_of(part * width + start, 128)
            pre[:, part * hidden : (part + 1) * hidden] += lax.dot_general(
                operand,
                roll[:, pl.ds(begin, tile)],
                CONTRACT_MINOR,
                preferred_element_type=jnp.float32,
            )

    dec_silu, unused_grad = silu_parts(pre[:, :hidden])
    act = (dec_silu * pre[:, hidden:]).astype(jnp.bfloat16)
    strip = 256 if out_width % 256 == 0 else 128
    for index in range(out_width // strip):
        begin = pl.multiple_of(2 * width + (1 - dp) * out_width + index * strip, 128)
        value = jnp.dot(act, roll[:, pl.ds(begin, strip)], preferred_element_type=jnp.float32)
        side_out[:, :, index * strip : (index + 1) * strip] = value.astype(jnp.bfloat16).reshape(
            pieces, -1, strip
        )
    order = list(range(pieces // 2, pieces)) + list(range(pieces // 2))
    side = [
        pltpu.make_async_remote_copy(
            src_ref=side_out.at[piece],
            dst_ref=side_in.at[piece],
            send_sem=side_send.at[piece],
            recv_sem=side_recv.at[piece],
            device_id={"group": group, "dp": 1 - dp},
            device_id_type=MESH,
        )
        for piece in range(pieces)
    ]
    for piece in order:
        side[piece].start()
    for index in range(out_width // strip):
        begin = pl.multiple_of(2 * width + dp * out_width + index * strip, 128)
        value = jnp.dot(act, roll[:, pl.ds(begin, strip)], preferred_element_type=jnp.float32)
        own[:, :, index * strip : (index + 1) * strip] = value.reshape(pieces, -1, strip)
    back = {}
    for piece in order:
        side[piece].wait_recv()
        total = (own[piece] + side_in[piece].astype(jnp.float32)).astype(jnp.bfloat16)
        total = total.reshape(per_piece, slots, out_width)
        for place in range(per_piece):
            far, step = divmod(piece * per_piece + place, EXPERTS)
            if far == 0 and step == 0:
                back_in[0, 0] = total[place]
                continue
            back_out[far, step] = total[place]
            to_half = 1 - half if far else half
            back[far, step] = pltpu.make_async_remote_copy(
                src_ref=back_out.at[far, step],
                dst_ref=back_in.at[far, step],
                send_sem=back_send.at[far, step],
                recv_sem=back_recv.at[far, step],
                device_id={
                    "group": to_half * EXPERTS + lax.rem(expert + EXPERTS - step, EXPERTS),
                    "dp": dp,
                },
                device_id_type=MESH,
            )
            back[far, step].start()
    for copy in back.values():
        copy.wait_recv()
    total = (back_in[0].astype(jnp.float32) + back_in[1].astype(jnp.float32)).astype(jnp.bfloat16)
    total = total.reshape(EXPERTS * slots, out_width)
    ids = droutes[...]
    turned = jnp.where(ids < expert, ids + EXPERTS - expert, ids - expert)
    back_sel = one_hot_rows(EXPERTS * slots, decode_place(ids, step_rows, slots, turned))
    picked = lax.dot_general(
        back_sel, total, CONTRACT_MAJOR, preferred_element_type=jnp.float32
    )
    out[...] = (as_column(dscale[...]) * picked).astype(jnp.bfloat16)
    for copy in back.values():
        copy.wait_send()
    for copy in side:
        copy.wait_send()


def adam_kernel(grads, master, first, second, new_master, new_first, new_second, roll):
    grad = grads[...]
    moment = beta_one * first[...] + (1.0 - beta_one) * grad
    square = beta_two * second[...] + (1.0 - beta_two) * grad * grad
    correct_one = 1.0 - beta_one**step_count
    correct_two = 1.0 - beta_two**step_count
    held = master[...]
    update = moment / correct_one / (jnp.sqrt(square / correct_two) + adam_eps)
    value = held - adam_lr * (update + decay_rate * held)
    new_first[...] = moment
    new_second[...] = square
    new_master[...] = value
    roll[...] = value.astype(jnp.bfloat16)


def moved_rows(
    tokens,
    routes,
    gate_scale,
    cotangent,
    master,
    moment_one,
    moment_two,
    dec_tokens,
    dec_routes,
    dec_scale,
):
    groups = lax.axis_size("group")
    width = tokens.shape[1]
    hidden = master.shape[1]
    steps, dec_here = dec_tokens.shape[:2]
    slots = steps * DCAP
    tokens_here = tokens.shape[0]
    dec_line = dec_routes.reshape(1, steps * dec_here)
    master_rows = master[0]
    vmem = pl.BlockSpec(memory_space=pltpu.VMEM)
    anywhere = pl.BlockSpec(memory_space=pl.ANY)
    dma = pltpu.SemaphoreType.DMA
    rows_all = 2 * 2 * EXPERTS * 2 * CAP
    grads, drows = pl.pallas_call(
        functools.partial(learner_kernel, groups, dec_here),
        out_shape=(
            jax.ShapeDtypeStruct((3 * hidden, width), jnp.float32),
            jax.ShapeDtypeStruct((2, EXPERTS, slots, width), jnp.bfloat16),
        ),
        in_specs=[vmem] * 6 + [anywhere],
        out_specs=(anywhere, anywhere),
        scratch_shapes=[
            pltpu.VMEM((3 * hidden, width), jnp.float32),
            pltpu.VMEM((tokens_here, 1), jnp.float32),
            pltpu.VMEM((EXPERTS * 2 * CAP, 2 * tokens_here), jnp.bfloat16),
            pltpu.VMEM((EXPERTS * slots, steps * dec_here), jnp.bfloat16),
            pltpu.VMEM((EXPERTS, 2 * CAP, width), jnp.bfloat16),
            pltpu.VMEM((2, 2, EXPERTS, 2 * CAP, width), jnp.bfloat16),
            pltpu.VMEM((EXPERTS, slots, width), jnp.bfloat16),
            pltpu.VMEM((2, EXPERTS, slots, width), jnp.bfloat16),
            pltpu.VMEM((hidden, 3 * width), jnp.bfloat16),
            pltpu.VMEM((EXPERTS * 2 * CAP, 3 * hidden), jnp.float32),
            pltpu.VMEM((3 * hidden, EXPERTS * 2 * CAP), jnp.bfloat16),
            dma((EXPERTS,)),
            dma((EXPERTS,)),
            dma((EXPERTS,)),
            dma((EXPERTS,)),
            dma((2, EXPERTS)),
            dma((2, EXPERTS)),
            dma((EXPERTS,)),
            dma((EXPERTS,)),
            dma((EXPERTS // 2,)),
            dma((EXPERTS // 2,)),
            dma((EXPERTS // 2,)),
            dma((EXPERTS // 2,)),
            dma(()),
            dma((width // pick_tile(width),)),
        ],
        compiler_params=pltpu.CompilerParams(
            collective_id=0, has_side_effects=True, vmem_limit_bytes=56 * 2**20
        ),
        cost_estimate=pl.CostEstimate(
            flops=12 * rows_all * hidden * width,
            bytes_accessed=24 * hidden * width,
            transcendentals=rows_all * hidden,
        ),
        name="learner",
    )(
        tokens,
        cotangent,
        gate_scale.reshape(1, tokens_here),
        routes.reshape(1, tokens_here),
        dec_tokens.reshape(steps * dec_here, width),
        dec_line,
        master_rows,
    )
    lines = min(32, hidden)
    tall = hidden // lines
    block = pl.BlockSpec((lines, width), lambda line, part: (line, part))
    wide = jax.ShapeDtypeStruct((hidden, 3 * width), jnp.float32)
    master_new, moment_new, second_new, rollout = pl.pallas_call(
        adam_kernel,
        grid=(tall, 3),
        out_shape=(wide, wide, wide, jax.ShapeDtypeStruct(wide.shape, jnp.bfloat16)),
        in_specs=[
            pl.BlockSpec((lines, width), lambda line, part: (part * tall + line, 0)),
            block,
            block,
            block,
        ],
        out_specs=(block, block, block, block),
        compiler_params=pltpu.CompilerParams(vmem_limit_bytes=40 * 2**20),
        cost_estimate=pl.CostEstimate(
            flops=60 * hidden * width,
            bytes_accessed=90 * hidden * width,
            transcendentals=6 * hidden * width,
        ),
        name="adam",
    )(grads, master_rows, moment_one[0], moment_two[0])
    out_width = width // 2
    rows_dec = 2 * EXPERTS * slots
    pieces = 8
    dec_out = pl.pallas_call(
        functools.partial(decode_kernel, groups, dec_here),
        out_shape=jax.ShapeDtypeStruct((steps * dec_here, out_width), jnp.bfloat16),
        in_specs=[vmem] * 4,
        out_specs=vmem,
        scratch_shapes=[
            pltpu.VMEM((rows_dec, 2 * hidden), jnp.float32),
            pltpu.VMEM((pieces, rows_dec // pieces, out_width), jnp.float32),
            pltpu.VMEM((pieces, rows_dec // pieces, out_width), jnp.bfloat16),
            pltpu.VMEM((pieces, rows_dec // pieces, out_width), jnp.bfloat16),
            pltpu.VMEM((2, EXPERTS, slots, out_width), jnp.bfloat16),
            pltpu.VMEM((2, EXPERTS, slots, out_width), jnp.bfloat16),
            dma((pieces,)),
            dma((pieces,)),
            dma((2, EXPERTS)),
            dma((2, EXPERTS)),
        ],
        compiler_params=pltpu.CompilerParams(
            collective_id=1, has_side_effects=True, vmem_limit_bytes=40 * 2**20
        ),
        cost_estimate=pl.CostEstimate(
            flops=6 * rows_dec * hidden * width,
            bytes_accessed=6 * hidden * width,
            transcendentals=rows_dec * hidden,
        ),
        name="decode",
    )(
        drows.reshape(rows_dec, width),
        rollout,
        dec_line,
        dec_scale.reshape(1, steps * dec_here),
    )
    return (
        master_new[None],
        moment_new[None],
        second_new[None],
        dec_out.reshape(steps, dec_here, out_width),
    )


def solution(mesh):
    in_specs = (
        P(("group", "dp"), None),
        P(("group", "dp"), None),
        P(("group", "dp"), None),
        P(("group", "dp"), None),
        P("group", "dp", None),
        P("group", "dp", None),
        P("group", "dp", None),
        P(None, "group", None),
        P(None, "group", None),
        P(None, "group", None),
    )
    out_specs = (
        P("group", "dp", None),
        P("group", "dp", None),
        P("group", "dp", None),
        P(None, "group", "dp"),
    )
    in_place = mesh.shape["group"] == 2 * EXPERTS and mesh.shape["dp"] == 2
    body = moved_rows if in_place else shards
    return jax.shard_map(body, mesh=mesh, in_specs=in_specs, out_specs=out_specs, check_vma=False)
```

```python
import functools

import jax
import jax.numpy as jnp
from jax import lax
from jax.experimental import pallas as pl
from jax.experimental.pallas import tpu as pltpu
from jax.sharding import PartitionSpec as P

EXPERTS = 8
CAP = 24
DCAP = 4


adam_lr = 0.001
beta_one = 0.9
beta_two = 0.95
adam_eps = 1e-08
decay_rate = 0.1
step_count = 100.0


def shifted(value, axis, by):
    count = lax.axis_size(axis)
    return lax.ppermute(value, axis, [(i, (i + by) % count) for i in range(count)])


def silu_parts(values):
    sig = jax.nn.sigmoid(values)
    return (values * sig, sig * (1.0 + values * (1.0 - sig)))


def rank_within(route_ids, experts, axis_dim):
    onehot = (route_ids[..., None] == jnp.arange(experts, dtype=jnp.int32)).astype(jnp.int32)
    running = jnp.cumsum(onehot, axis=axis_dim) - 1
    return jnp.sum(running * onehot, axis=-1)


def send_rows(value):
    return lax.all_to_all(value, "group", split_axis=1, concat_axis=1, tiled=True)


def from_peers(value, experts, split, axis_dim):
    parts = [value]
    for offset in range(1, split):
        parts.append(shifted(value, "group", offset * experts))
    return jnp.concatenate(parts, axis_dim)


def contract_rows(left, right):
    return lax.dot_general(
        left, right, (((1,), (1,)), ((), ())), preferred_element_type=jnp.float32
    )


def shards(
    tokens,
    routes,
    gate_scale,
    cotangent,
    master,
    moment_one,
    moment_two,
    dec_tokens,
    dec_routes,
    dec_scale,
):
    groups = lax.axis_size("group")
    replicas = lax.axis_size("dp")
    experts = EXPERTS
    split = groups // experts
    width = tokens.shape[1]
    capacity = CAP
    route_ids = routes[:, 0]
    slot_index = rank_within(route_ids, experts, 0)
    scaled = (gate_scale * cotangent.astype(jnp.float32)).astype(jnp.bfloat16)
    position = route_ids * capacity + slot_index
    select = (jnp.arange(experts * capacity, dtype=jnp.int32)[:, None] == position[None, :]).astype(
        jnp.bfloat16
    )
    packed = jnp.stack(
        [
            jnp.dot(select, tokens, preferred_element_type=jnp.float32),
            jnp.dot(select, scaled, preferred_element_type=jnp.float32),
        ],
        0,
    ).astype(jnp.bfloat16)
    packed = packed.reshape(2, 1, experts * capacity, width)
    tiled = jnp.broadcast_to(packed, (2, split, experts * capacity, width)).reshape(
        2, groups, capacity, width
    )
    arrived = send_rows(tiled)
    row_data = arrived.reshape(2, groups * capacity, width)
    x_rows = row_data[0]
    d_rows = row_data[1]
    master_rows = master[0]
    slice_w = lax.all_gather(master_rows.astype(jnp.bfloat16), "dp", axis=0, tiled=True)
    gate_pre = contract_rows(x_rows, slice_w[:, :width])
    up_pre = contract_rows(x_rows, slice_w[:, width : 2 * width])
    back_pre = contract_rows(d_rows, slice_w[:, 2 * width :])
    silu_val, silu_grad = silu_parts(gate_pre)
    activated = (silu_val * up_pre).astype(jnp.bfloat16)
    grad_up = (back_pre * silu_val).astype(jnp.bfloat16)
    grad_gate = (back_pre * up_pre * silu_grad).astype(jnp.bfloat16)
    pieces = []
    for source, operand in ((grad_gate, x_rows), (grad_up, x_rows), (activated, d_rows)):
        pieces.append(
            lax.dot_general(
                source, operand, (((0,), (0,)), ((), ())), preferred_element_type=jnp.float32
            )
        )
    grads = lax.psum_scatter(jnp.concatenate(pieces, 1), "dp", scatter_dimension=0, tiled=True)
    moment_new = beta_one * moment_one[0] + (1.0 - beta_one) * grads
    second_new = beta_two * moment_two[0] + (1.0 - beta_two) * grads * grads
    correct_one = 1.0 - beta_one**step_count
    correct_two = 1.0 - beta_two**step_count
    update = moment_new / correct_one / (jnp.sqrt(second_new / correct_two) + adam_eps)
    master_new = master_rows - adam_lr * (update + decay_rate * master_rows)
    rollout = from_peers(master_new.astype(jnp.bfloat16), experts, split, 0)
    per_peer = DCAP // split
    out_width = width // replicas
    own_index = lax.axis_index("group")
    outputs = []
    for step_index in range(dec_tokens.shape[0]):
        inputs = dec_tokens[step_index : step_index + 1]
        steps_here = inputs.shape[0]
        ids_now = dec_routes[step_index : step_index + 1][..., 0]
        slot_now = rank_within(ids_now, experts, 1)
        block_now = (slot_now // per_peer + own_index) % split
        decode_position = (
            block_now * (experts * per_peer) + ids_now * per_peer + slot_now % per_peer
        )
        decode_select = (
            jnp.arange(groups * per_peer, dtype=jnp.int32)[None, :, None]
            == decode_position[:, None, :]
        ).astype(jnp.bfloat16)
        decode_packed = jnp.einsum(
            "spr,srd->spd", decode_select, inputs, preferred_element_type=jnp.float32
        ).astype(jnp.bfloat16)
        decode_arrived = send_rows(decode_packed.reshape(steps_here, groups, per_peer, width))
        dec_rows = decode_arrived.reshape(steps_here * groups * per_peer, width)
        dec_gate = contract_rows(dec_rows, rollout[:, :width])
        dec_up = contract_rows(dec_rows, rollout[:, width : 2 * width])
        dec_silu, unused_grad = silu_parts(dec_gate)
        dec_act = (dec_silu * dec_up).astype(jnp.bfloat16)
        down_columns = lax.dynamic_slice_in_dim(
            rollout, 2 * width, out_width * lax.axis_size("dp"), 1
        )
        summed = lax.psum_scatter(
            lax.dot_general(
                down_columns, dec_act, (((0,), (1,)), ((), ())), preferred_element_type=jnp.float32
            ),
            "dp",
            scatter_dimension=0,
            tiled=True,
        )
        expert_out = summed.T.astype(jnp.bfloat16).reshape(steps_here, groups, per_peer, out_width)
        returned = send_rows(expert_out).reshape(steps_here, groups * per_peer, out_width)
        picked = jnp.einsum(
            "spr,spd->srd", decode_select, returned, preferred_element_type=jnp.float32
        )
        outputs.append((dec_scale[step_index : step_index + 1] * picked).astype(jnp.bfloat16))
    dec_out = jnp.concatenate(outputs, 0)
    return (master_new[None], moment_new[None], second_new[None], dec_out)


MESH = pl.DeviceIdType.MESH
PIECES = 4
CONTRACT_MINOR = (((1,), (1,)), ((), ()))
CONTRACT_MAJOR = (((0,), (0,)), ((), ()))


def pick_tile(width):
    return 512 if width % 512 == 0 else 128


def count_before(ids, group_of):
    count = ids.shape[1]
    lines = lax.broadcasted_iota(jnp.int32, (16, count), 0)
    onehot = (lines == ids).astype(jnp.float32)
    earlier = lax.broadcasted_iota(jnp.int32, (count, count), 0)
    later = lax.broadcasted_iota(jnp.int32, (count, count), 1)
    before = (earlier < later) & (earlier // group_of == later // group_of)
    running = jnp.dot(
        onehot.astype(jnp.bfloat16),
        before.astype(jnp.float32).astype(jnp.bfloat16),
        preferred_element_type=jnp.float32,
    )
    return jnp.sum(running * onehot, axis=0, keepdims=True)


def as_column(line):
    count = line.shape[1]
    across = lax.broadcasted_iota(jnp.int32, (count, count), 0)
    along = lax.broadcasted_iota(jnp.int32, (count, count), 1)
    return jnp.sum(jnp.where(across == along, line, 0.0), axis=1, keepdims=True)


def one_hot_rows(count, place):
    lines = lax.broadcasted_iota(jnp.int32, (count, place.shape[1]), 0).astype(jnp.float32)
    return (lines == place).astype(jnp.float32).astype(jnp.bfloat16)


def decode_place(ids, step_rows, slots, turned):
    step_of = lax.broadcasted_iota(jnp.int32, ids.shape, 1) // step_rows
    within = (step_of * DCAP).astype(jnp.float32) + count_before(ids, step_rows)
    return (turned * slots).astype(jnp.float32) + within


def greet_peers(own_group, own_dp, groups):
    barrier = pltpu.get_barrier_semaphore()
    for step in range(1, groups):
        pl.semaphore_signal(
            barrier,
            inc=1,
            device_id={"group": lax.rem(own_group + step, groups), "dp": own_dp},
            device_id_type=MESH,
        )
    pl.semaphore_signal(
        barrier, inc=1, device_id={"group": own_group, "dp": 1 - own_dp}, device_id_type=MESH
    )


def await_peers(groups):
    pl.semaphore_wait(pltpu.get_barrier_semaphore(), groups)


def learner_kernel(
    groups,
    step_rows,
    tok,
    cot,
    scale_line,
    routes,
    dtok,
    droutes,
    master,
    grads_out,
    drows_out,
    grads,
    rounded,
    gate_scale,
    sel,
    far_sel,
    dsel,
    raw,
    far_raw,
    ids_out,
    ids_in,
    packed,
    far_packed,
    rows,
    dpacked,
    drows,
    weights,
    pre,
    left,
    raw_send,
    raw_recv,
    ids_send,
    ids_recv,
    near_send,
    near_recv,
    far_send,
    far_recv,
    side_send,
    side_recv,
    far_side_send,
    far_side_recv,
    dnear_send,
    dnear_recv,
    dhalf_send,
    dhalf_recv,
    out_sem,
    grads_sem,
):
    group = lax.axis_index("group")
    dp = lax.axis_index("dp")
    half = group // EXPERTS
    expert = lax.rem(group, EXPERTS)
    count, width = tok.shape
    hidden = weights.shape[0]
    tile = pick_tile(width)
    block = 2 * CAP
    chunk = EXPERTS * block
    piece = width // PIECES
    spans = [pl.ds(index * piece, piece) for index in range(PIECES)]

    def remote(src, dst, send, recv, to_group, to_dp):
        return pltpu.make_async_remote_copy(
            src_ref=src,
            dst_ref=dst,
            send_sem=send,
            recv_sem=recv,
            device_id={"group": to_group, "dp": to_dp},
            device_id_type=MESH,
        )

    def slots_of(ids):
        place = (ids * block).astype(jnp.float32) + count_before(ids, count)
        return one_hot_rows(chunk, jnp.concatenate([place, place + CAP], 1))

    greet_peers(group, dp, groups)
    gate_scale[...] = as_column(scale_line[...])
    ids_out[...] = jnp.broadcast_to(routes[...].astype(jnp.float32), ids_out.shape).astype(
        jnp.bfloat16
    )
    raw[:count] = tok[...]

    @pl.loop(0, width // tile)
    def _(index):
        columns = pl.ds(pl.multiple_of(index * tile, tile), tile)
        raw[count:, columns] = (gate_scale[...] * cot[:, columns].astype(jnp.float32)).astype(
            jnp.bfloat16
        )

    await_peers(groups)
    other_group = (1 - half) * EXPERTS + expert
    ids_copy = remote(ids_out, ids_in, ids_send, ids_recv, other_group, dp)
    ids_copy.start()
    across = [
        remote(
            raw.at[:, spans[index]],
            far_raw.at[:, spans[index]],
            raw_send.at[index],
            raw_recv.at[index],
            other_group,
            dp,
        )
        for index in range(PIECES)
    ]
    for copy in across:
        copy.start()

    sel[...] = slots_of(routes[...])

    @pl.loop(0, width // tile)
    def _(index):
        columns = pl.ds(pl.multiple_of(index * tile, tile), tile)
        picked = jnp.dot(sel[...], raw[:, columns], preferred_element_type=jnp.float32)
        packed[:, :, columns] = picked.astype(jnp.bfloat16).reshape(EXPERTS, block, tile)

    def peer(step):
        return half * EXPERTS + lax.rem(expert + step, EXPERTS)

    near = [None] + [
        remote(
            packed.at[lax.rem(expert + step, EXPERTS)],
            rows.at[0, 0, step],
            near_send.at[step],
            near_recv.at[step],
            peer(step),
            dp,
        )
        for step in range(1, EXPERTS)
    ]
    beside = [
        remote(
            packed.at[expert] if step == 0 else rows.at[0, 0, step],
            rows.at[1, 0, step],
            side_send.at[step],
            side_recv.at[step],
            group,
            1 - dp,
        )
        for step in range(EXPERTS)
    ]
    far_near = {}
    further = {}
    for index in range(PIECES):
        for step in range(EXPERTS):
            if step:
                far_near[index, step] = remote(
                    far_packed.at[lax.rem(expert + step, EXPERTS), :, spans[index]],
                    rows.at[0, 1, step, :, spans[index]],
                    far_send.at[index, step],
                    far_recv.at[index, step],
                    peer(step),
                    dp,
                )
            further[index, step] = remote(
                rows.at[0, 1, step, :, spans[index]],
                rows.at[1, 1, step, :, spans[index]],
                far_side_send.at[index, step],
                far_side_recv.at[index, step],
                group,
                1 - dp,
            )
    dnear = [None] + [
        remote(
            dpacked.at[lax.rem(expert + step, EXPERTS)],
            drows.at[0, step],
            dnear_send.at[step],
            dnear_recv.at[step],
            peer(step),
            dp,
        )
        for step in range(1, EXPERTS)
    ]
    dacross = [
        remote(
            dpacked.at[lax.rem(expert + step, EXPERTS)],
            drows.at[1, step],
            dhalf_send.at[step],
            dhalf_recv.at[step],
            (1 - half) * EXPERTS + lax.rem(expert + step, EXPERTS),
            dp,
        )
        for step in range(EXPERTS)
    ]

    beside[0].start()
    for step in range(1, EXPERTS):
        near[step].start()
    rows[0, 0, 0] = packed[expert]

    slots = dpacked.shape[1]
    ids = droutes[...]
    dsel[...] = one_hot_rows(EXPERTS * slots, decode_place(ids, step_rows, slots, ids))

    @pl.loop(0, width // tile)
    def _(index):
        columns = pl.ds(pl.multiple_of(index * tile, tile), tile)
        picked = jnp.dot(dsel[...], dtok[:, columns], preferred_element_type=jnp.float32)
        dpacked[:, :, columns] = picked.astype(jnp.bfloat16).reshape(EXPERTS, -1, tile)

    drows[0, 0] = dpacked[expert]
    lines = min(16, hidden)

    def cast_body(source):
        begin = pl.multiple_of(pl.program_id(0) * lines, lines)
        weights[pl.ds(begin, lines), :] = source[...].astype(jnp.bfloat16)

    pltpu.emit_pipeline(
        cast_body,
        grid=(hidden // lines,),
        in_specs=[pl.BlockSpec((lines, 3 * width), lambda i: (i, 0))],
        out_specs=[],
    )(master)

    for step in range(1, EXPERTS):
        near[step].wait_recv()
        beside[step].start()

    def score(own, start, size):
        operand = own[:, :, pl.ds(start, size)].reshape(chunk, size)
        for part in range(3):
            pre[:, part * hidden : (part + 1) * hidden] += lax.dot_general(
                operand,
                weights[:, pl.ds(pl.multiple_of(part * width + start, 128), size)],
                CONTRACT_MINOR,
                preferred_element_type=jnp.float32,
            )

    def score_all(own):
        pre[...] = jnp.zeros_like(pre)

        @pl.loop(0, width // tile)
        def _(index):
            score(own, pl.multiple_of(index * tile, tile), tile)

    def accumulate(own, first=False, last=False):
        parts = pre[...].reshape(EXPERTS, block, 3 * hidden)
        gate_pre = parts[:, :CAP, :hidden]
        up_pre = parts[:, :CAP, hidden : 2 * hidden]
        back_pre = parts[:, CAP:, 2 * hidden :]
        silu_val, silu_grad = silu_parts(gate_pre)
        zeros = jnp.zeros_like(gate_pre)
        top = jnp.concatenate([back_pre * up_pre * silu_grad, back_pre * silu_val, zeros], 2)
        bottom = jnp.concatenate([zeros, zeros, silu_val * up_pre], 2)
        left[...] = (
            jnp.concatenate([top, bottom], 1)
            .reshape(chunk, 3 * hidden)
            .T.astype(jnp.bfloat16)
        )

        @pl.loop(0, width // tile)
        def _(index):
            columns = pl.ds(pl.multiple_of(index * tile, tile), tile)
            operand = own[:, :, columns].reshape(chunk, tile)
            value = jnp.dot(left[...], operand, preferred_element_type=jnp.float32)
            if first:
                grads[:, columns] = value
            elif last:
                rounded[:, columns] = (grads[:, columns] + value).astype(jnp.bfloat16)
                pltpu.make_async_copy(
                    rounded.at[:, columns], grads_out.at[:, columns], grads_sem.at[index]
                ).start()
            else:
                grads[:, columns] += value

    def spread(index):
        across[index].wait_recv()
        if index == 0:
            ids_copy.wait_recv()
            far_sel[...] = slots_of(ids_in[0:1, :].astype(jnp.float32).astype(jnp.int32))
        picked = jnp.dot(
            far_sel[...], far_raw[:, spans[index]], preferred_element_type=jnp.float32
        )
        far_packed[:, :, spans[index]] = picked.astype(jnp.bfloat16).reshape(
            EXPERTS, block, piece
        )
        for step in range(1, EXPERTS):
            far_near[index, step].start()
        rows[0, 1, 0, :, spans[index]] = far_packed[expert, :, spans[index]]
        further[index, 0].start()

    def pass_on(index):
        for step in range(1, EXPERTS):
            far_near[index, step].wait_recv()
            further[index, step].start()

    spread(0)
    own = rows.at[0, 0]
    score_all(own)
    accumulate(own, first=True)
    pass_on(0)
    for index in range(1, PIECES):
        spread(index)
        if index == PIECES - 1:
            for step in range(EXPERTS):
                dacross[step].start()
            for step in range(1, EXPERTS):
                dnear[step].start()
        pass_on(index)
        if index == PIECES - 2:
            for step in range(EXPERTS):
                beside[step].wait_recv()
            own = rows.at[1, 0]
            score_all(own)
            accumulate(own)
    own = rows.at[0, 1]
    score_all(own)
    accumulate(own)
    own = rows.at[1, 1]
    pre[...] = jnp.zeros_like(pre)
    for index in range(PIECES):
        for step in range(EXPERTS):
            further[index, step].wait_recv()
        score(own, index * piece, piece)
    accumulate(own, last=True)
    for step in range(EXPERTS):
        dacross[step].wait_recv()
        if step:
            dnear[step].wait_recv()
    leave = pltpu.make_async_copy(drows, drows_out, out_sem)
    leave.start()

    @pl.loop(0, width // tile)
    def _(index):
        columns = pl.ds(pl.multiple_of(index * tile, tile), tile)
        pltpu.make_async_copy(
            rounded.at[:, columns], grads_out.at[:, columns], grads_sem.at[index]
        ).wait()

    leave.wait()
    ids_copy.wait_send()
    for copy in across + beside + near[1:] + dnear[1:] + dacross:
        copy.wait_send()
    for copy in far_near.values():
        copy.wait_send()
    for copy in further.values():
        copy.wait_send()


def decode_kernel(
    groups,
    step_rows,
    drows_in,
    roll_in,
    droutes,
    dscale,
    out,
    drows,
    roll,
    pre,
    own,
    side_out,
    side_in,
    back_out,
    back_in,
    side_send,
    side_recv,
    back_send,
    back_recv,
    in_sem,
):
    group = lax.axis_index("group")
    dp = lax.axis_index("dp")
    half = group // EXPERTS
    expert = lax.rem(group, EXPERTS)
    hidden, wide = roll.shape
    width = wide // 3
    out_width = width // 2
    tile = pick_tile(width)
    slots = drows.shape[0] // (2 * EXPERTS)
    pieces = side_out.shape[0]
    per_piece = 2 * EXPERTS // pieces
    fetches = [
        pltpu.make_async_copy(drows_in, drows, in_sem.at[0]),
        pltpu.make_async_copy(
            roll_in.at[:, : 2 * width], roll.at[:, : 2 * width], in_sem.at[1]
        ),
        pltpu.make_async_copy(
            roll_in.at[:, 2 * width :], roll.at[:, 2 * width :], in_sem.at[2]
        ),
    ]
    for fetch in fetches:
        fetch.start()
    greet_peers(group, dp, groups)
    pre[...] = jnp.zeros_like(pre)
    fetches[0].wait()
    fetches[1].wait()

    @pl.loop(0, width // tile)
    def _(index):
        start = pl.multiple_of(index * tile, tile)
        operand = drows[:, pl.ds(start, tile)]
        for part in range(2):
            begin = pl.multiple_of(part * width + start, 128)
            pre[:, part * hidden : (part + 1) * hidden] += lax.dot_general(
                operand,
                roll[:, pl.ds(begin, tile)],
                CONTRACT_MINOR,
                preferred_element_type=jnp.float32,
            )

    dec_silu, unused_grad = silu_parts(pre[:, :hidden])
    act = (dec_silu * pre[:, hidden:]).astype(jnp.bfloat16)
    fetches[2].wait()
    strip = 256 if out_width % 256 == 0 else 128
    for index in range(out_width // strip):
        begin = pl.multiple_of(2 * width + (1 - dp) * out_width + index * strip, 128)
        value = jnp.dot(act, roll[:, pl.ds(begin, strip)], preferred_element_type=jnp.float32)
        side_out[:, :, index * strip : (index + 1) * strip] = value.astype(jnp.bfloat16).reshape(
            pieces, -1, strip
        )
    order = list(range(pieces // 2, pieces)) + list(range(pieces // 2))
    side = [
        pltpu.make_async_remote_copy(
            src_ref=side_out.at[piece],
            dst_ref=side_in.at[piece],
            send_sem=side_send.at[piece],
            recv_sem=side_recv.at[piece],
            device_id={"group": group, "dp": 1 - dp},
            device_id_type=MESH,
        )
        for piece in range(pieces)
    ]
    await_peers(groups)
    for piece in order:
        side[piece].start()
    for index in range(out_width // strip):
        begin = pl.multiple_of(2 * width + dp * out_width + index * strip, 128)
        value = jnp.dot(act, roll[:, pl.ds(begin, strip)], preferred_element_type=jnp.float32)
        own[:, :, index * strip : (index + 1) * strip] = value.reshape(pieces, -1, strip)
    back = {}
    for piece in order:
        side[piece].wait_recv()
        total = (own[piece] + side_in[piece].astype(jnp.float32)).astype(jnp.bfloat16)
        total = total.reshape(per_piece, slots, out_width)
        for place in range(per_piece):
            far, step = divmod(piece * per_piece + place, EXPERTS)
            if far == 0 and step == 0:
                back_in[0, 0] = total[place]
                continue
            back_out[far, step] = total[place]
            to_half = 1 - half if far else half
            back[far, step] = pltpu.make_async_remote_copy(
                src_ref=back_out.at[far, step],
                dst_ref=back_in.at[far, step],
                send_sem=back_send.at[far, step],
                recv_sem=back_recv.at[far, step],
                device_id={
                    "group": to_half * EXPERTS + lax.rem(expert + EXPERTS - step, EXPERTS),
                    "dp": dp,
                },
                device_id_type=MESH,
            )
            back[far, step].start()
    for copy in back.values():
        copy.wait_recv()
    total = (back_in[0].astype(jnp.float32) + back_in[1].astype(jnp.float32)).astype(jnp.bfloat16)
    total = total.reshape(EXPERTS * slots, out_width)
    ids = droutes[...]
    turned = jnp.where(ids < expert, ids + EXPERTS - expert, ids - expert)
    back_sel = one_hot_rows(EXPERTS * slots, decode_place(ids, step_rows, slots, turned))
    picked = lax.dot_general(
        back_sel, total, CONTRACT_MAJOR, preferred_element_type=jnp.float32
    )
    out[...] = (as_column(dscale[...]) * picked).astype(jnp.bfloat16)
    for copy in back.values():
        copy.wait_send()
    for copy in side:
        copy.wait_send()


def adam_kernel(grads, master, first, second, new_master, new_first, new_second, roll):
    grad = grads[...].astype(jnp.float32)
    moment = beta_one * first[...] + (1.0 - beta_one) * grad
    square = beta_two * second[...] + (1.0 - beta_two) * grad * grad
    scale_one = adam_lr / (1.0 - beta_one**step_count)
    scale_two = 1.0 / (1.0 - beta_two**step_count)
    corrected = square * scale_two
    root = corrected * lax.rsqrt(corrected) + adam_eps
    value = (1.0 - adam_lr * decay_rate) * master[...] - (scale_one * moment) / root
    new_first[...] = moment
    new_second[...] = square
    new_master[...] = value
    roll[...] = value.astype(jnp.bfloat16)


def moved_rows(
    tokens,
    routes,
    gate_scale,
    cotangent,
    master,
    moment_one,
    moment_two,
    dec_tokens,
    dec_routes,
    dec_scale,
):
    groups = lax.axis_size("group")
    width = tokens.shape[1]
    hidden = master.shape[1]
    steps, dec_here = dec_tokens.shape[:2]
    slots = steps * DCAP
    tokens_here = tokens.shape[0]
    dec_line = dec_routes.reshape(1, steps * dec_here)
    master_rows = master[0]
    vmem = pl.BlockSpec(memory_space=pltpu.VMEM)
    anywhere = pl.BlockSpec(memory_space=pl.ANY)
    dma = pltpu.SemaphoreType.DMA
    rows_all = 2 * 2 * EXPERTS * 2 * CAP
    grads, drows = pl.pallas_call(
        functools.partial(learner_kernel, groups, dec_here),
        out_shape=(
            jax.ShapeDtypeStruct((3 * hidden, width), jnp.bfloat16),
            jax.ShapeDtypeStruct((2, EXPERTS, slots, width), jnp.bfloat16),
        ),
        in_specs=[vmem] * 6 + [anywhere],
        out_specs=(anywhere, anywhere),
        scratch_shapes=[
            pltpu.VMEM((3 * hidden, width), jnp.float32),
            pltpu.VMEM((3 * hidden, width), jnp.bfloat16),
            pltpu.VMEM((tokens_here, 1), jnp.float32),
            pltpu.VMEM((EXPERTS * 2 * CAP, 2 * tokens_here), jnp.bfloat16),
            pltpu.VMEM((EXPERTS * 2 * CAP, 2 * tokens_here), jnp.bfloat16),
            pltpu.VMEM((EXPERTS * slots, steps * dec_here), jnp.bfloat16),
            pltpu.VMEM((2 * tokens_here, width), jnp.bfloat16),
            pltpu.VMEM((2 * tokens_here, width), jnp.bfloat16),
            pltpu.VMEM((16, tokens_here), jnp.bfloat16),
            pltpu.VMEM((16, tokens_here), jnp.bfloat16),
            pltpu.VMEM((EXPERTS, 2 * CAP, width), jnp.bfloat16),
            pltpu.VMEM((EXPERTS, 2 * CAP, width), jnp.bfloat16),
            pltpu.VMEM((2, 2, EXPERTS, 2 * CAP, width), jnp.bfloat16),
            pltpu.VMEM((EXPERTS, slots, width), jnp.bfloat16),
            pltpu.VMEM((2, EXPERTS, slots, width), jnp.bfloat16),
            pltpu.VMEM((hidden, 3 * width), jnp.bfloat16),
            pltpu.VMEM((EXPERTS * 2 * CAP, 3 * hidden), jnp.float32),
            pltpu.VMEM((3 * hidden, EXPERTS * 2 * CAP), jnp.bfloat16),
            dma((PIECES,)),
            dma((PIECES,)),
            dma(()),
            dma(()),
            dma((EXPERTS,)),
            dma((EXPERTS,)),
            dma((PIECES, EXPERTS)),
            dma((PIECES, EXPERTS)),
            dma((EXPERTS,)),
            dma((EXPERTS,)),
            dma((PIECES, EXPERTS)),
            dma((PIECES, EXPERTS)),
            dma((EXPERTS,)),
            dma((EXPERTS,)),
            dma((EXPERTS,)),
            dma((EXPERTS,)),
            dma(()),
            dma((width // pick_tile(width),)),
        ],
        compiler_params=pltpu.CompilerParams(
            collective_id=0, has_side_effects=True, vmem_limit_bytes=56 * 2**20
        ),
        cost_estimate=pl.CostEstimate(
            flops=12 * rows_all * hidden * width,
            bytes_accessed=24 * hidden * width,
            transcendentals=rows_all * hidden,
        ),
        name="learner",
    )(
        tokens,
        cotangent,
        gate_scale.reshape(1, tokens_here),
        routes.reshape(1, tokens_here),
        dec_tokens.reshape(steps * dec_here, width),
        dec_line,
        master_rows,
    )
    lines = min(32, hidden)
    tall = hidden // lines
    block = pl.BlockSpec((lines, width), lambda line, part: (line, part))
    wide = jax.ShapeDtypeStruct((hidden, 3 * width), jnp.float32)
    master_new, moment_new, second_new, rollout = pl.pallas_call(
        adam_kernel,
        grid=(tall, 3),
        out_shape=(wide, wide, wide, jax.ShapeDtypeStruct(wide.shape, jnp.bfloat16)),
        in_specs=[
            pl.BlockSpec((lines, width), lambda line, part: (part * tall + line, 0)),
            block,
            block,
            block,
        ],
        out_specs=(block, block, block, block),
        compiler_params=pltpu.CompilerParams(vmem_limit_bytes=40 * 2**20),
        cost_estimate=pl.CostEstimate(
            flops=60 * hidden * width,
            bytes_accessed=90 * hidden * width,
            transcendentals=6 * hidden * width,
        ),
        name="adam",
    )(grads, master_rows, moment_one[0], moment_two[0])
    out_width = width // 2
    rows_dec = 2 * EXPERTS * slots
    pieces = 8
    dec_out = pl.pallas_call(
        functools.partial(decode_kernel, groups, dec_here),
        out_shape=jax.ShapeDtypeStruct((steps * dec_here, out_width), jnp.bfloat16),
        in_specs=[anywhere, anywhere, vmem, vmem],
        out_specs=vmem,
        scratch_shapes=[
            pltpu.VMEM((rows_dec, width), jnp.bfloat16),
            pltpu.VMEM((hidden, 3 * width), jnp.bfloat16),
            pltpu.VMEM((rows_dec, 2 * hidden), jnp.float32),
            pltpu.VMEM((pieces, rows_dec // pieces, out_width), jnp.float32),
            pltpu.VMEM((pieces, rows_dec // pieces, out_width), jnp.bfloat16),
            pltpu.VMEM((pieces, rows_dec // pieces, out_width), jnp.bfloat16),
            pltpu.VMEM((2, EXPERTS, slots, out_width), jnp.bfloat16),
            pltpu.VMEM((2, EXPERTS, slots, out_width), jnp.bfloat16),
            dma((pieces,)),
            dma((pieces,)),
            dma((2, EXPERTS)),
            dma((2, EXPERTS)),
            dma((3,)),
        ],
        compiler_params=pltpu.CompilerParams(
            collective_id=1, has_side_effects=True, vmem_limit_bytes=56 * 2**20
        ),
        cost_estimate=pl.CostEstimate(
            flops=6 * rows_dec * hidden * width,
            bytes_accessed=6 * hidden * width,
            transcendentals=rows_dec * hidden,
        ),
        name="decode",
    )(
        drows.reshape(rows_dec, width),
        rollout,
        dec_line,
        dec_scale.reshape(1, steps * dec_here),
    )
    return (
        master_new[None],
        moment_new[None],
        second_new[None],
        dec_out.reshape(steps, dec_here, out_width),
    )


def solution(mesh):
    in_specs = (
        P(("group", "dp"), None),
        P(("group", "dp"), None),
        P(("group", "dp"), None),
        P(("group", "dp"), None),
        P("group", "dp", None),
        P("group", "dp", None),
        P("group", "dp", None),
        P(None, "group", None),
        P(None, "group", None),
        P(None, "group", None),
    )
    out_specs = (
        P("group", "dp", None),
        P("group", "dp", None),
        P("group", "dp", None),
        P(None, "group", "dp"),
    )
    in_place = mesh.shape["group"] == 2 * EXPERTS and mesh.shape["dp"] == 2
    body = moved_rows if in_place else shards
    return jax.shard_map(body, mesh=mesh, in_specs=in_specs, out_specs=out_specs, check_vma=False)
```

```python
import functools

import jax
import jax.numpy as jnp
from jax import lax
from jax.experimental import pallas as pl
from jax.experimental.pallas import tpu as pltpu
from jax.sharding import PartitionSpec as P

EXPERTS = 8
CAP = 24
DCAP = 4


adam_lr = 0.001
beta_one = 0.9
beta_two = 0.95
adam_eps = 1e-08
decay_rate = 0.1
step_count = 100.0


def shifted(value, axis, by):
    count = lax.axis_size(axis)
    return lax.ppermute(value, axis, [(i, (i + by) % count) for i in range(count)])


def silu_parts(values):
    sig = jax.nn.sigmoid(values)
    return (values * sig, sig * (1.0 + values * (1.0 - sig)))


def rank_within(route_ids, experts, axis_dim):
    onehot = (route_ids[..., None] == jnp.arange(experts, dtype=jnp.int32)).astype(jnp.int32)
    running = jnp.cumsum(onehot, axis=axis_dim) - 1
    return jnp.sum(running * onehot, axis=-1)


def send_rows(value):
    return lax.all_to_all(value, "group", split_axis=1, concat_axis=1, tiled=True)


def from_peers(value, experts, split, axis_dim):
    parts = [value]
    for offset in range(1, split):
        parts.append(shifted(value, "group", offset * experts))
    return jnp.concatenate(parts, axis_dim)


def contract_rows(left, right):
    return lax.dot_general(
        left, right, (((1,), (1,)), ((), ())), preferred_element_type=jnp.float32
    )


def shards(
    tokens,
    routes,
    gate_scale,
    cotangent,
    master,
    moment_one,
    moment_two,
    dec_tokens,
    dec_routes,
    dec_scale,
):
    groups = lax.axis_size("group")
    replicas = lax.axis_size("dp")
    experts = EXPERTS
    split = groups // experts
    width = tokens.shape[1]
    capacity = CAP
    route_ids = routes[:, 0]
    slot_index = rank_within(route_ids, experts, 0)
    scaled = (gate_scale * cotangent.astype(jnp.float32)).astype(jnp.bfloat16)
    position = route_ids * capacity + slot_index
    select = (jnp.arange(experts * capacity, dtype=jnp.int32)[:, None] == position[None, :]).astype(
        jnp.bfloat16
    )
    packed = jnp.stack(
        [
            jnp.dot(select, tokens, preferred_element_type=jnp.float32),
            jnp.dot(select, scaled, preferred_element_type=jnp.float32),
        ],
        0,
    ).astype(jnp.bfloat16)
    packed = packed.reshape(2, 1, experts * capacity, width)
    tiled = jnp.broadcast_to(packed, (2, split, experts * capacity, width)).reshape(
        2, groups, capacity, width
    )
    arrived = send_rows(tiled)
    row_data = arrived.reshape(2, groups * capacity, width)
    x_rows = row_data[0]
    d_rows = row_data[1]
    master_rows = master[0]
    slice_w = lax.all_gather(master_rows.astype(jnp.bfloat16), "dp", axis=0, tiled=True)
    gate_pre = contract_rows(x_rows, slice_w[:, :width])
    up_pre = contract_rows(x_rows, slice_w[:, width : 2 * width])
    back_pre = contract_rows(d_rows, slice_w[:, 2 * width :])
    silu_val, silu_grad = silu_parts(gate_pre)
    activated = (silu_val * up_pre).astype(jnp.bfloat16)
    grad_up = (back_pre * silu_val).astype(jnp.bfloat16)
    grad_gate = (back_pre * up_pre * silu_grad).astype(jnp.bfloat16)
    pieces = []
    for source, operand in ((grad_gate, x_rows), (grad_up, x_rows), (activated, d_rows)):
        pieces.append(
            lax.dot_general(
                source, operand, (((0,), (0,)), ((), ())), preferred_element_type=jnp.float32
            )
        )
    grads = lax.psum_scatter(jnp.concatenate(pieces, 1), "dp", scatter_dimension=0, tiled=True)
    moment_new = beta_one * moment_one[0] + (1.0 - beta_one) * grads
    second_new = beta_two * moment_two[0] + (1.0 - beta_two) * grads * grads
    correct_one = 1.0 - beta_one**step_count
    correct_two = 1.0 - beta_two**step_count
    update = moment_new / correct_one / (jnp.sqrt(second_new / correct_two) + adam_eps)
    master_new = master_rows - adam_lr * (update + decay_rate * master_rows)
    rollout = from_peers(master_new.astype(jnp.bfloat16), experts, split, 0)
    per_peer = DCAP // split
    out_width = width // replicas
    own_index = lax.axis_index("group")
    outputs = []
    for step_index in range(dec_tokens.shape[0]):
        inputs = dec_tokens[step_index : step_index + 1]
        steps_here = inputs.shape[0]
        ids_now = dec_routes[step_index : step_index + 1][..., 0]
        slot_now = rank_within(ids_now, experts, 1)
        block_now = (slot_now // per_peer + own_index) % split
        decode_position = (
            block_now * (experts * per_peer) + ids_now * per_peer + slot_now % per_peer
        )
        decode_select = (
            jnp.arange(groups * per_peer, dtype=jnp.int32)[None, :, None]
            == decode_position[:, None, :]
        ).astype(jnp.bfloat16)
        decode_packed = jnp.einsum(
            "spr,srd->spd", decode_select, inputs, preferred_element_type=jnp.float32
        ).astype(jnp.bfloat16)
        decode_arrived = send_rows(decode_packed.reshape(steps_here, groups, per_peer, width))
        dec_rows = decode_arrived.reshape(steps_here * groups * per_peer, width)
        dec_gate = contract_rows(dec_rows, rollout[:, :width])
        dec_up = contract_rows(dec_rows, rollout[:, width : 2 * width])
        dec_silu, unused_grad = silu_parts(dec_gate)
        dec_act = (dec_silu * dec_up).astype(jnp.bfloat16)
        down_columns = lax.dynamic_slice_in_dim(
            rollout, 2 * width, out_width * lax.axis_size("dp"), 1
        )
        summed = lax.psum_scatter(
            lax.dot_general(
                down_columns, dec_act, (((0,), (1,)), ((), ())), preferred_element_type=jnp.float32
            ),
            "dp",
            scatter_dimension=0,
            tiled=True,
        )
        expert_out = summed.T.astype(jnp.bfloat16).reshape(steps_here, groups, per_peer, out_width)
        returned = send_rows(expert_out).reshape(steps_here, groups * per_peer, out_width)
        picked = jnp.einsum(
            "spr,spd->srd", decode_select, returned, preferred_element_type=jnp.float32
        )
        outputs.append((dec_scale[step_index : step_index + 1] * picked).astype(jnp.bfloat16))
    dec_out = jnp.concatenate(outputs, 0)
    return (master_new[None], moment_new[None], second_new[None], dec_out)


MESH = pl.DeviceIdType.MESH
PIECES = 4
CONTRACT_MINOR = (((1,), (1,)), ((), ()))
CONTRACT_MAJOR = (((0,), (0,)), ((), ()))


def pick_tile(width):
    return 512 if width % 512 == 0 else 128


def count_before(ids, group_of):
    count = ids.shape[1]
    lines = lax.broadcasted_iota(jnp.int32, (16, count), 0)
    onehot = (lines == ids).astype(jnp.float32)
    earlier = lax.broadcasted_iota(jnp.int32, (count, count), 0)
    later = lax.broadcasted_iota(jnp.int32, (count, count), 1)
    before = (earlier < later) & (earlier // group_of == later // group_of)
    running = jnp.dot(
        onehot.astype(jnp.bfloat16),
        before.astype(jnp.float32).astype(jnp.bfloat16),
        preferred_element_type=jnp.float32,
    )
    return jnp.sum(running * onehot, axis=0, keepdims=True)


def in_line(ref):
    return jnp.concatenate([ref[index] for index in range(ref.shape[0])], 1)


def as_column(line):
    count = line.shape[1]
    across = lax.broadcasted_iota(jnp.int32, (count, count), 0)
    along = lax.broadcasted_iota(jnp.int32, (count, count), 1)
    return jnp.sum(jnp.where(across == along, line, 0.0), axis=1, keepdims=True)


def one_hot_rows(count, place):
    lines = lax.broadcasted_iota(jnp.int32, (count, place.shape[1]), 0).astype(jnp.float32)
    return (lines == place).astype(jnp.float32).astype(jnp.bfloat16)


def decode_place(ids, step_rows, slots, turned):
    step_of = lax.broadcasted_iota(jnp.int32, ids.shape, 1) // step_rows
    within = (step_of * DCAP).astype(jnp.float32) + count_before(ids, step_rows)
    return (turned * slots).astype(jnp.float32) + within


def greet_peers(own_group, own_dp, groups):
    barrier = pltpu.get_barrier_semaphore()
    for step in range(1, groups):
        pl.semaphore_signal(
            barrier,
            inc=1,
            device_id={"group": lax.rem(own_group + step, groups), "dp": own_dp},
            device_id_type=MESH,
        )
    pl.semaphore_signal(
        barrier, inc=1, device_id={"group": own_group, "dp": 1 - own_dp}, device_id_type=MESH
    )
    twin = own_group + 1 - 2 * lax.rem(own_group, 2)
    pl.semaphore_signal(
        barrier, inc=1, device_id={"group": twin, "dp": 1 - own_dp}, device_id_type=MESH
    )


def await_peers(groups):
    pl.semaphore_wait(pltpu.get_barrier_semaphore(), groups + 1)


def learner_kernel(
    groups,
    step_rows,
    tok,
    cot,
    scale_line,
    routes,
    dtok,
    droutes,
    master,
    grads_out,
    drows_out,
    grads,
    rounded,
    gate_scale,
    sel,
    far_sel,
    dsel,
    raw,
    far_raw,
    ids_out,
    ids_in,
    packed,
    far_packed,
    rows,
    dpacked,
    drows,
    weights,
    pre,
    left,
    raw_send,
    raw_recv,
    ids_send,
    ids_recv,
    near_send,
    near_recv,
    far_send,
    far_recv,
    side_send,
    side_recv,
    far_side_send,
    far_side_recv,
    dnear_send,
    dnear_recv,
    dhalf_send,
    dhalf_recv,
    out_sem,
    grads_sem,
):
    group = lax.axis_index("group")
    dp = lax.axis_index("dp")
    half = group // EXPERTS
    expert = lax.rem(group, EXPERTS)
    count, width = tok.shape
    hidden = weights.shape[0]
    tile = pick_tile(width)
    block = 2 * CAP
    chunk = EXPERTS * block
    piece = width // PIECES
    spans = [pl.ds(index * piece, piece) for index in range(PIECES)]

    def remote(src, dst, send, recv, to_group, to_dp):
        return pltpu.make_async_remote_copy(
            src_ref=src,
            dst_ref=dst,
            send_sem=send,
            recv_sem=recv,
            device_id={"group": to_group, "dp": to_dp},
            device_id_type=MESH,
        )

    def slots_of(ids):
        place = (ids * block).astype(jnp.float32) + count_before(ids, count)
        return one_hot_rows(chunk, jnp.concatenate([place, place + CAP], 1))

    greet_peers(group, dp, groups)
    gate_scale[...] = as_column(scale_line[...])
    ids_out[...] = jnp.broadcast_to(routes[...].astype(jnp.float32), ids_out.shape).astype(
        jnp.bfloat16
    )
    raw[:count] = tok[...]

    @pl.loop(0, width // tile)
    def _(index):
        columns = pl.ds(pl.multiple_of(index * tile, tile), tile)
        raw[count:, columns] = (gate_scale[...] * cot[:, columns].astype(jnp.float32)).astype(
            jnp.bfloat16
        )

    await_peers(groups)
    other_group = (1 - half) * EXPERTS + expert
    ids_copy = remote(ids_out, ids_in, ids_send, ids_recv, other_group, dp)
    ids_copy.start()
    across = [
        remote(
            raw.at[:, spans[index]],
            far_raw.at[:, spans[index]],
            raw_send.at[index],
            raw_recv.at[index],
            other_group,
            dp,
        )
        for index in range(PIECES)
    ]
    for copy in across:
        copy.start()

    sel[...] = slots_of(routes[...])

    @pl.loop(0, width // tile)
    def _(index):
        columns = pl.ds(pl.multiple_of(index * tile, tile), tile)
        picked = jnp.dot(sel[...], raw[:, columns], preferred_element_type=jnp.float32)
        packed[:, :, columns] = picked.astype(jnp.bfloat16).reshape(EXPERTS, block, tile)

    def peer(step):
        return half * EXPERTS + lax.rem(expert + step, EXPERTS)

    near = [None] + [
        remote(
            packed.at[lax.rem(expert + step, EXPERTS)],
            rows.at[0, 0, step],
            near_send.at[step],
            near_recv.at[step],
            peer(step),
            dp,
        )
        for step in range(1, EXPERTS)
    ]
    beside = [
        remote(
            packed.at[expert] if step == 0 else rows.at[0, 0, step],
            rows.at[1, 0, step],
            side_send.at[step],
            side_recv.at[step],
            group,
            1 - dp,
        )
        for step in range(EXPERTS)
    ]
    far_near = {}
    further = {}
    for index in range(PIECES):
        for step in range(EXPERTS):
            if step:
                far_near[index, step] = remote(
                    far_packed.at[lax.rem(expert + step, EXPERTS), :, spans[index]],
                    rows.at[0, 1, step, :, spans[index]],
                    far_send.at[index, step],
                    far_recv.at[index, step],
                    peer(step),
                    dp,
                )
            further[index, step] = remote(
                rows.at[0, 1, step, :, spans[index]],
                rows.at[1, 1, step, :, spans[index]],
                far_side_send.at[index, step],
                far_side_recv.at[index, step],
                group,
                1 - dp,
            )
    dnear = [None] + [
        remote(
            dpacked.at[lax.rem(expert + step, EXPERTS)],
            drows.at[0, step],
            dnear_send.at[step],
            dnear_recv.at[step],
            peer(step),
            dp,
        )
        for step in range(1, EXPERTS)
    ]
    dacross = [
        remote(
            dpacked.at[lax.rem(expert + step, EXPERTS)],
            drows.at[1, step],
            dhalf_send.at[step],
            dhalf_recv.at[step],
            (1 - half) * EXPERTS + lax.rem(expert + step, EXPERTS),
            dp,
        )
        for step in range(EXPERTS)
    ]

    twin = jnp.where(lax.rem(expert, 2) == 0, 1, EXPERTS - 1)
    mirror = EXPERTS - twin
    beside[0].start()
    remote(
        packed.at[lax.rem(expert + twin, EXPERTS)],
        rows.at[1, 0, twin],
        side_send.at[mirror],
        side_recv.at[twin],
        peer(twin),
        1 - dp,
    ).start()
    for step in range(1, EXPERTS):
        near[step].start()
    rows[0, 0, 0] = packed[expert]

    slots = dpacked.shape[1]
    ids = in_line(droutes)
    dsel[...] = one_hot_rows(EXPERTS * slots, decode_place(ids, step_rows, slots, ids))

    @pl.loop(0, width // tile)
    def _(index):
        columns = pl.ds(pl.multiple_of(index * tile, tile), tile)
        picked = jnp.dot(dsel[...], dtok[:, columns], preferred_element_type=jnp.float32)
        dpacked[:, :, columns] = picked.astype(jnp.bfloat16).reshape(EXPERTS, -1, tile)

    drows[0, 0] = dpacked[expert]
    lines = min(16, hidden)

    def cast_body(source):
        begin = pl.multiple_of(pl.program_id(0) * lines, lines)
        weights[pl.ds(begin, lines), :] = source[...].astype(jnp.bfloat16)

    pltpu.emit_pipeline(
        cast_body,
        grid=(hidden // lines,),
        in_specs=[pl.BlockSpec((lines, 3 * width), lambda i: (i, 0))],
        out_specs=[],
    )(master)

    near[1].wait_recv()
    near[EXPERTS - 1].wait_recv()
    remote(
        rows.at[0, 0, twin],
        rows.at[1, 0, twin],
        side_send.at[twin],
        side_recv.at[twin],
        group,
        1 - dp,
    ).start()
    for step in range(2, EXPERTS - 1):
        near[step].wait_recv()
        beside[step].start()

    def score(own, start, size):
        operand = own[:, :, pl.ds(start, size)].reshape(chunk, size)
        for part in range(3):
            pre[:, part * hidden : (part + 1) * hidden] += lax.dot_general(
                operand,
                weights[:, pl.ds(pl.multiple_of(part * width + start, 128), size)],
                CONTRACT_MINOR,
                preferred_element_type=jnp.float32,
            )

    def score_all(own):
        pre[...] = jnp.zeros_like(pre)

        @pl.loop(0, width // tile)
        def _(index):
            score(own, pl.multiple_of(index * tile, tile), tile)

    def accumulate(own, first=False, last=False):
        parts = pre[...].reshape(EXPERTS, block, 3 * hidden)
        gate_pre = parts[:, :CAP, :hidden]
        up_pre = parts[:, :CAP, hidden : 2 * hidden]
        back_pre = parts[:, CAP:, 2 * hidden :]
        silu_val, silu_grad = silu_parts(gate_pre)
        zeros = jnp.zeros_like(gate_pre)
        top = jnp.concatenate([back_pre * up_pre * silu_grad, back_pre * silu_val, zeros], 2)
        bottom = jnp.concatenate([zeros, zeros, silu_val * up_pre], 2)
        left[...] = (
            jnp.concatenate([top, bottom], 1)
            .reshape(chunk, 3 * hidden)
            .T.astype(jnp.bfloat16)
        )

        @pl.loop(0, width // tile)
        def _(index):
            columns = pl.ds(pl.multiple_of(index * tile, tile), tile)
            operand = own[:, :, columns].reshape(chunk, tile)
            value = jnp.dot(left[...], operand, preferred_element_type=jnp.float32)
            if first:
                grads[:, columns] = value
            elif last:
                rounded[:, columns] = (grads[:, columns] + value).astype(jnp.bfloat16)
                pltpu.make_async_copy(
                    rounded.at[:, columns], grads_out.at[:, columns], grads_sem.at[index]
                ).start()
            else:
                grads[:, columns] += value

    def spread(index):
        across[index].wait_recv()
        if index == 0:
            ids_copy.wait_recv()
            far_sel[...] = slots_of(ids_in[0:1, :].astype(jnp.float32).astype(jnp.int32))
        picked = jnp.dot(
            far_sel[...], far_raw[:, spans[index]], preferred_element_type=jnp.float32
        )
        far_packed[:, :, spans[index]] = picked.astype(jnp.bfloat16).reshape(
            EXPERTS, block, piece
        )
        for step in range(1, EXPERTS):
            far_near[index, step].start()
        rows[0, 1, 0, :, spans[index]] = far_packed[expert, :, spans[index]]
        further[index, 0].start()

    def pass_on(index):
        for step in range(1, EXPERTS):
            far_near[index, step].wait_recv()
            further[index, step].start()

    spread(0)
    own = rows.at[0, 0]
    score_all(own)
    accumulate(own, first=True)
    pass_on(0)
    for index in range(1, PIECES):
        spread(index)
        if index == PIECES - 1:
            for step in range(EXPERTS):
                dacross[step].start()
            for step in range(1, EXPERTS):
                dnear[step].start()
        pass_on(index)
        if index == PIECES - 2:
            for step in range(EXPERTS):
                beside[step].wait_recv()
            own = rows.at[1, 0]
            score_all(own)
            accumulate(own)
    own = rows.at[0, 1]
    score_all(own)
    accumulate(own)
    own = rows.at[1, 1]
    pre[...] = jnp.zeros_like(pre)
    for index in range(PIECES):
        for step in range(EXPERTS):
            further[index, step].wait_recv()
        score(own, index * piece, piece)
    accumulate(own, last=True)
    for step in range(EXPERTS):
        dacross[step].wait_recv()
        if step:
            dnear[step].wait_recv()
    leave = pltpu.make_async_copy(drows, drows_out, out_sem)
    leave.start()

    @pl.loop(0, width // tile)
    def _(index):
        columns = pl.ds(pl.multiple_of(index * tile, tile), tile)
        pltpu.make_async_copy(
            rounded.at[:, columns], grads_out.at[:, columns], grads_sem.at[index]
        ).wait()

    leave.wait()
    ids_copy.wait_send()
    for copy in across + beside + near[1:] + dnear[1:] + dacross:
        copy.wait_send()
    for copy in far_near.values():
        copy.wait_send()
    for copy in further.values():
        copy.wait_send()


def decode_kernel(
    groups,
    step_rows,
    drows_in,
    roll_in,
    droutes,
    dscale,
    out,
    drows,
    roll,
    pre,
    own,
    side_out,
    side_in,
    back_out,
    back_in,
    side_send,
    side_recv,
    back_send,
    back_recv,
    in_sem,
):
    group = lax.axis_index("group")
    dp = lax.axis_index("dp")
    half = group // EXPERTS
    expert = lax.rem(group, EXPERTS)
    hidden, wide = roll.shape
    width = wide // 3
    out_width = width // 2
    tile = pick_tile(width)
    slots = drows.shape[0] // (2 * EXPERTS)
    pieces = side_out.shape[0]
    per_piece = 2 * EXPERTS // pieces
    fetches = [
        pltpu.make_async_copy(drows_in, drows, in_sem.at[0]),
        pltpu.make_async_copy(
            roll_in.at[:, : 2 * width], roll.at[:, : 2 * width], in_sem.at[1]
        ),
        pltpu.make_async_copy(
            roll_in.at[:, 2 * width :], roll.at[:, 2 * width :], in_sem.at[2]
        ),
    ]
    for fetch in fetches:
        fetch.start()
    greet_peers(group, dp, groups)
    pre[...] = jnp.zeros_like(pre)
    fetches[0].wait()
    fetches[1].wait()

    @pl.loop(0, width // tile)
    def _(index):
        start = pl.multiple_of(index * tile, tile)
        operand = drows[:, pl.ds(start, tile)]
        for part in range(2):
            begin = pl.multiple_of(part * width + start, 128)
            pre[:, part * hidden : (part + 1) * hidden] += lax.dot_general(
                operand,
                roll[:, pl.ds(begin, tile)],
                CONTRACT_MINOR,
                preferred_element_type=jnp.float32,
            )

    dec_silu, unused_grad = silu_parts(pre[:, :hidden])
    act = (dec_silu * pre[:, hidden:]).astype(jnp.bfloat16)
    fetches[2].wait()
    strip = 256 if out_width % 256 == 0 else 128
    for index in range(out_width // strip):
        begin = pl.multiple_of(2 * width + (1 - dp) * out_width + index * strip, 128)
        value = jnp.dot(act, roll[:, pl.ds(begin, strip)], preferred_element_type=jnp.float32)
        side_out[:, :, index * strip : (index + 1) * strip] = value.astype(jnp.bfloat16).reshape(
            pieces, -1, strip
        )
    order = list(range(pieces // 2, pieces)) + list(range(pieces // 2))
    side = [
        pltpu.make_async_remote_copy(
            src_ref=side_out.at[piece],
            dst_ref=side_in.at[piece],
            send_sem=side_send.at[piece],
            recv_sem=side_recv.at[piece],
            device_id={"group": group, "dp": 1 - dp},
            device_id_type=MESH,
        )
        for piece in range(pieces)
    ]
    await_peers(groups)
    for piece in order:
        side[piece].start()
    for index in range(out_width // strip):
        begin = pl.multiple_of(2 * width + dp * out_width + index * strip, 128)
        value = jnp.dot(act, roll[:, pl.ds(begin, strip)], preferred_element_type=jnp.float32)
        own[:, :, index * strip : (index + 1) * strip] = value.reshape(pieces, -1, strip)
    back = {}
    for piece in order:
        side[piece].wait_recv()
        total = (own[piece] + side_in[piece].astype(jnp.float32)).astype(jnp.bfloat16)
        total = total.reshape(per_piece, slots, out_width)
        for place in range(per_piece):
            far, step = divmod(piece * per_piece + place, EXPERTS)
            if far == 0 and step == 0:
                back_in[0, 0] = total[place]
                continue
            back_out[far, step] = total[place]
            to_half = 1 - half if far else half
            back[far, step] = pltpu.make_async_remote_copy(
                src_ref=back_out.at[far, step],
                dst_ref=back_in.at[far, step],
                send_sem=back_send.at[far, step],
                recv_sem=back_recv.at[far, step],
                device_id={
                    "group": to_half * EXPERTS + lax.rem(expert + EXPERTS - step, EXPERTS),
                    "dp": dp,
                },
                device_id_type=MESH,
            )
            back[far, step].start()
    for copy in back.values():
        copy.wait_recv()
    total = (back_in[0].astype(jnp.float32) + back_in[1].astype(jnp.float32)).astype(jnp.bfloat16)
    total = total.reshape(EXPERTS * slots, out_width)
    ids = in_line(droutes)
    turned = jnp.where(ids < expert, ids + EXPERTS - expert, ids - expert)
    back_sel = one_hot_rows(EXPERTS * slots, decode_place(ids, step_rows, slots, turned))
    picked = lax.dot_general(
        back_sel, total, CONTRACT_MAJOR, preferred_element_type=jnp.float32
    )
    out[...] = (as_column(in_line(dscale)) * picked).astype(jnp.bfloat16)
    for copy in back.values():
        copy.wait_send()
    for copy in side:
        copy.wait_send()


def adam_kernel(grads, master, first, second, new_master, new_first, new_second, roll):
    grad = grads[...].astype(jnp.float32)
    moment = beta_one * first[...] + (1.0 - beta_one) * grad
    square = beta_two * second[...] + (1.0 - beta_two) * grad * grad
    scale_one = adam_lr / (1.0 - beta_one**step_count)
    scale_two = 1.0 / (1.0 - beta_two**step_count)
    corrected = square * scale_two
    root = corrected * lax.rsqrt(corrected) + adam_eps
    value = (1.0 - adam_lr * decay_rate) * master[...] - (scale_one * moment) / root
    new_first[...] = moment
    new_second[...] = square
    new_master[...] = value
    roll[...] = value.astype(jnp.bfloat16)


def moved_rows(
    tokens,
    routes,
    gate_scale,
    cotangent,
    master,
    moment_one,
    moment_two,
    dec_tokens,
    dec_routes,
    dec_scale,
):
    groups = lax.axis_size("group")
    width = tokens.shape[1]
    hidden = master.shape[1]
    steps, dec_here = dec_tokens.shape[:2]
    slots = steps * DCAP
    tokens_here = tokens.shape[0]
    dec_line = jnp.transpose(dec_routes, (0, 2, 1))
    master_rows = master[0]
    vmem = pl.BlockSpec(memory_space=pltpu.VMEM)
    anywhere = pl.BlockSpec(memory_space=pl.ANY)
    dma = pltpu.SemaphoreType.DMA
    rows_all = 2 * 2 * EXPERTS * 2 * CAP
    grads, drows = pl.pallas_call(
        functools.partial(learner_kernel, groups, dec_here),
        out_shape=(
            jax.ShapeDtypeStruct((3 * hidden, width), jnp.bfloat16),
            jax.ShapeDtypeStruct((2, EXPERTS, slots, width), jnp.bfloat16),
        ),
        in_specs=[vmem] * 6 + [anywhere],
        out_specs=(anywhere, anywhere),
        scratch_shapes=[
            pltpu.VMEM((3 * hidden, width), jnp.float32),
            pltpu.VMEM((3 * hidden, width), jnp.bfloat16),
            pltpu.VMEM((tokens_here, 1), jnp.float32),
            pltpu.VMEM((EXPERTS * 2 * CAP, 2 * tokens_here), jnp.bfloat16),
            pltpu.VMEM((EXPERTS * 2 * CAP, 2 * tokens_here), jnp.bfloat16),
            pltpu.VMEM((EXPERTS * slots, steps * dec_here), jnp.bfloat16),
            pltpu.VMEM((2 * tokens_here, width), jnp.bfloat16),
            pltpu.VMEM((2 * tokens_here, width), jnp.bfloat16),
            pltpu.VMEM((16, tokens_here), jnp.bfloat16),
            pltpu.VMEM((16, tokens_here), jnp.bfloat16),
            pltpu.VMEM((EXPERTS, 2 * CAP, width), jnp.bfloat16),
            pltpu.VMEM((EXPERTS, 2 * CAP, width), jnp.bfloat16),
            pltpu.VMEM((2, 2, EXPERTS, 2 * CAP, width), jnp.bfloat16),
            pltpu.VMEM((EXPERTS, slots, width), jnp.bfloat16),
            pltpu.VMEM((2, EXPERTS, slots, width), jnp.bfloat16),
            pltpu.VMEM((hidden, 3 * width), jnp.bfloat16),
            pltpu.VMEM((EXPERTS * 2 * CAP, 3 * hidden), jnp.float32),
            pltpu.VMEM((3 * hidden, EXPERTS * 2 * CAP), jnp.bfloat16),
            dma((PIECES,)),
            dma((PIECES,)),
            dma(()),
            dma(()),
            dma((EXPERTS,)),
            dma((EXPERTS,)),
            dma((PIECES, EXPERTS)),
            dma((PIECES, EXPERTS)),
            dma((EXPERTS,)),
            dma((EXPERTS,)),
            dma((PIECES, EXPERTS)),
            dma((PIECES, EXPERTS)),
            dma((EXPERTS,)),
            dma((EXPERTS,)),
            dma((EXPERTS,)),
            dma((EXPERTS,)),
            dma(()),
            dma((width // pick_tile(width),)),
        ],
        compiler_params=pltpu.CompilerParams(
            collective_id=0, has_side_effects=True, vmem_limit_bytes=56 * 2**20
        ),
        cost_estimate=pl.CostEstimate(
            flops=12 * rows_all * hidden * width,
            bytes_accessed=24 * hidden * width,
            transcendentals=rows_all * hidden,
        ),
        name="learner",
    )(
        tokens,
        cotangent,
        gate_scale.reshape(1, tokens_here),
        routes.reshape(1, tokens_here),
        dec_tokens.reshape(steps * dec_here, width),
        dec_line,
        master_rows,
    )
    lines = min(32, hidden)
    tall = hidden // lines
    block = pl.BlockSpec((lines, width), lambda line, part: (line, part))
    wide = jax.ShapeDtypeStruct((hidden, 3 * width), jnp.float32)
    master_new, moment_new, second_new, rollout = pl.pallas_call(
        adam_kernel,
        grid=(tall, 3),
        out_shape=(wide, wide, wide, jax.ShapeDtypeStruct(wide.shape, jnp.bfloat16)),
        in_specs=[
            pl.BlockSpec((lines, width), lambda line, part: (part * tall + line, 0)),
            block,
            block,
            block,
        ],
        out_specs=(block, block, block, block),
        compiler_params=pltpu.CompilerParams(vmem_limit_bytes=56 * 2**20),
        cost_estimate=pl.CostEstimate(
            flops=60 * hidden * width,
            bytes_accessed=90 * hidden * width,
            transcendentals=6 * hidden * width,
        ),
        name="adam",
    )(grads, master_rows, moment_one[0], moment_two[0])
    out_width = width // 2
    rows_dec = 2 * EXPERTS * slots
    pieces = 8
    dec_out = pl.pallas_call(
        functools.partial(decode_kernel, groups, dec_here),
        out_shape=jax.ShapeDtypeStruct((steps * dec_here, out_width), jnp.bfloat16),
        in_specs=[anywhere, anywhere, vmem, vmem],
        out_specs=vmem,
        scratch_shapes=[
            pltpu.VMEM((rows_dec, width), jnp.bfloat16),
            pltpu.VMEM((hidden, 3 * width), jnp.bfloat16),
            pltpu.VMEM((rows_dec, 2 * hidden), jnp.float32),
            pltpu.VMEM((pieces, rows_dec // pieces, out_width), jnp.float32),
            pltpu.VMEM((pieces, rows_dec // pieces, out_width), jnp.bfloat16),
            pltpu.VMEM((pieces, rows_dec // pieces, out_width), jnp.bfloat16),
            pltpu.VMEM((2, EXPERTS, slots, out_width), jnp.bfloat16),
            pltpu.VMEM((2, EXPERTS, slots, out_width), jnp.bfloat16),
            dma((pieces,)),
            dma((pieces,)),
            dma((2, EXPERTS)),
            dma((2, EXPERTS)),
            dma((3,)),
        ],
        compiler_params=pltpu.CompilerParams(
            collective_id=1, has_side_effects=True, vmem_limit_bytes=56 * 2**20
        ),
        cost_estimate=pl.CostEstimate(
            flops=6 * rows_dec * hidden * width,
            bytes_accessed=6 * hidden * width,
            transcendentals=rows_dec * hidden,
        ),
        name="decode",
    )(
        drows.reshape(rows_dec, width),
        rollout,
        dec_line,
        jnp.transpose(dec_scale, (0, 2, 1)),
    )
    return (
        master_new[None],
        moment_new[None],
        second_new[None],
        dec_out.reshape(steps, dec_here, out_width),
    )


def solution(mesh):
    in_specs = (
        P(("group", "dp"), None),
        P(("group", "dp"), None),
        P(("group", "dp"), None),
        P(("group", "dp"), None),
        P("group", "dp", None),
        P("group", "dp", None),
        P("group", "dp", None),
        P(None, "group", None),
        P(None, "group", None),
        P(None, "group", None),
    )
    out_specs = (
        P("group", "dp", None),
        P("group", "dp", None),
        P("group", "dp", None),
        P(None, "group", "dp"),
    )
    in_place = mesh.shape["group"] == 2 * EXPERTS and mesh.shape["dp"] == 2
    body = moved_rows if in_place else shards
    return jax.shard_map(body, mesh=mesh, in_specs=in_specs, out_specs=out_specs, check_vma=False)
```

```python
import functools

import jax
import jax.numpy as jnp
from jax import lax
from jax.experimental import pallas as pl
from jax.experimental.pallas import tpu as pltpu
from jax.sharding import PartitionSpec as P

EXPERTS = 8
CAP = 24
DCAP = 4


adam_lr = 0.001
beta_one = 0.9
beta_two = 0.95
adam_eps = 1e-08
decay_rate = 0.1
step_count = 100.0


def shifted(value, axis, by):
    count = lax.axis_size(axis)
    return lax.ppermute(value, axis, [(i, (i + by) % count) for i in range(count)])


def silu_parts(values):
    sig = jax.nn.sigmoid(values)
    return (values * sig, sig * (1.0 + values * (1.0 - sig)))


def rank_within(route_ids, experts, axis_dim):
    onehot = (route_ids[..., None] == jnp.arange(experts, dtype=jnp.int32)).astype(jnp.int32)
    running = jnp.cumsum(onehot, axis=axis_dim) - 1
    return jnp.sum(running * onehot, axis=-1)


def send_rows(value):
    return lax.all_to_all(value, "group", split_axis=1, concat_axis=1, tiled=True)


def from_peers(value, experts, split, axis_dim):
    parts = [value]
    for offset in range(1, split):
        parts.append(shifted(value, "group", offset * experts))
    return jnp.concatenate(parts, axis_dim)


def contract_rows(left, right):
    return lax.dot_general(
        left, right, (((1,), (1,)), ((), ())), preferred_element_type=jnp.float32
    )


def shards(
    tokens,
    routes,
    gate_scale,
    cotangent,
    master,
    moment_one,
    moment_two,
    dec_tokens,
    dec_routes,
    dec_scale,
):
    groups = lax.axis_size("group")
    replicas = lax.axis_size("dp")
    experts = EXPERTS
    split = groups // experts
    width = tokens.shape[1]
    capacity = CAP
    route_ids = routes[:, 0]
    slot_index = rank_within(route_ids, experts, 0)
    scaled = (gate_scale * cotangent.astype(jnp.float32)).astype(jnp.bfloat16)
    position = route_ids * capacity + slot_index
    select = (jnp.arange(experts * capacity, dtype=jnp.int32)[:, None] == position[None, :]).astype(
        jnp.bfloat16
    )
    packed = jnp.stack(
        [
            jnp.dot(select, tokens, preferred_element_type=jnp.float32),
            jnp.dot(select, scaled, preferred_element_type=jnp.float32),
        ],
        0,
    ).astype(jnp.bfloat16)
    packed = packed.reshape(2, 1, experts * capacity, width)
    tiled = jnp.broadcast_to(packed, (2, split, experts * capacity, width)).reshape(
        2, groups, capacity, width
    )
    arrived = send_rows(tiled)
    row_data = arrived.reshape(2, groups * capacity, width)
    x_rows = row_data[0]
    d_rows = row_data[1]
    master_rows = master[0]
    slice_w = lax.all_gather(master_rows.astype(jnp.bfloat16), "dp", axis=0, tiled=True)
    gate_pre = contract_rows(x_rows, slice_w[:, :width])
    up_pre = contract_rows(x_rows, slice_w[:, width : 2 * width])
    back_pre = contract_rows(d_rows, slice_w[:, 2 * width :])
    silu_val, silu_grad = silu_parts(gate_pre)
    activated = (silu_val * up_pre).astype(jnp.bfloat16)
    grad_up = (back_pre * silu_val).astype(jnp.bfloat16)
    grad_gate = (back_pre * up_pre * silu_grad).astype(jnp.bfloat16)
    pieces = []
    for source, operand in ((grad_gate, x_rows), (grad_up, x_rows), (activated, d_rows)):
        pieces.append(
            lax.dot_general(
                source, operand, (((0,), (0,)), ((), ())), preferred_element_type=jnp.float32
            )
        )
    grads = lax.psum_scatter(jnp.concatenate(pieces, 1), "dp", scatter_dimension=0, tiled=True)
    moment_new = beta_one * moment_one[0] + (1.0 - beta_one) * grads
    second_new = beta_two * moment_two[0] + (1.0 - beta_two) * grads * grads
    correct_one = 1.0 - beta_one**step_count
    correct_two = 1.0 - beta_two**step_count
    update = moment_new / correct_one / (jnp.sqrt(second_new / correct_two) + adam_eps)
    master_new = master_rows - adam_lr * (update + decay_rate * master_rows)
    rollout = from_peers(master_new.astype(jnp.bfloat16), experts, split, 0)
    per_peer = DCAP // split
    out_width = width // replicas
    own_index = lax.axis_index("group")
    outputs = []
    for step_index in range(dec_tokens.shape[0]):
        inputs = dec_tokens[step_index : step_index + 1]
        steps_here = inputs.shape[0]
        ids_now = dec_routes[step_index : step_index + 1][..., 0]
        slot_now = rank_within(ids_now, experts, 1)
        block_now = (slot_now // per_peer + own_index) % split
        decode_position = (
            block_now * (experts * per_peer) + ids_now * per_peer + slot_now % per_peer
        )
        decode_select = (
            jnp.arange(groups * per_peer, dtype=jnp.int32)[None, :, None]
            == decode_position[:, None, :]
        ).astype(jnp.bfloat16)
        decode_packed = jnp.einsum(
            "spr,srd->spd", decode_select, inputs, preferred_element_type=jnp.float32
        ).astype(jnp.bfloat16)
        decode_arrived = send_rows(decode_packed.reshape(steps_here, groups, per_peer, width))
        dec_rows = decode_arrived.reshape(steps_here * groups * per_peer, width)
        dec_gate = contract_rows(dec_rows, rollout[:, :width])
        dec_up = contract_rows(dec_rows, rollout[:, width : 2 * width])
        dec_silu, unused_grad = silu_parts(dec_gate)
        dec_act = (dec_silu * dec_up).astype(jnp.bfloat16)
        down_columns = lax.dynamic_slice_in_dim(
            rollout, 2 * width, out_width * lax.axis_size("dp"), 1
        )
        summed = lax.psum_scatter(
            lax.dot_general(
                down_columns, dec_act, (((0,), (1,)), ((), ())), preferred_element_type=jnp.float32
            ),
            "dp",
            scatter_dimension=0,
            tiled=True,
        )
        expert_out = summed.T.astype(jnp.bfloat16).reshape(steps_here, groups, per_peer, out_width)
        returned = send_rows(expert_out).reshape(steps_here, groups * per_peer, out_width)
        picked = jnp.einsum(
            "spr,spd->srd", decode_select, returned, preferred_element_type=jnp.float32
        )
        outputs.append((dec_scale[step_index : step_index + 1] * picked).astype(jnp.bfloat16))
    dec_out = jnp.concatenate(outputs, 0)
    return (master_new[None], moment_new[None], second_new[None], dec_out)


MESH = pl.DeviceIdType.MESH
PIECES = 4
CONTRACT_MINOR = (((1,), (1,)), ((), ()))
CONTRACT_MAJOR = (((0,), (0,)), ((), ()))


def pick_tile(width):
    return 512 if width % 512 == 0 else 128


def count_before(ids, group_of):
    count = ids.shape[1]
    lines = lax.broadcasted_iota(jnp.int32, (16, count), 0)
    onehot = (lines == ids).astype(jnp.float32)
    earlier = lax.broadcasted_iota(jnp.int32, (count, count), 0)
    later = lax.broadcasted_iota(jnp.int32, (count, count), 1)
    before = (earlier < later) & (earlier // group_of == later // group_of)
    running = jnp.dot(
        onehot.astype(jnp.bfloat16),
        before.astype(jnp.float32).astype(jnp.bfloat16),
        preferred_element_type=jnp.float32,
    )
    return jnp.sum(running * onehot, axis=0, keepdims=True)


def in_line(ref):
    return jnp.concatenate([ref[index] for index in range(ref.shape[0])], 1)


def as_column(line):
    count = line.shape[1]
    across = lax.broadcasted_iota(jnp.int32, (count, count), 0)
    along = lax.broadcasted_iota(jnp.int32, (count, count), 1)
    return jnp.sum(jnp.where(across == along, line, 0.0), axis=1, keepdims=True)


def one_hot_rows(count, place):
    lines = lax.broadcasted_iota(jnp.int32, (count, place.shape[1]), 0).astype(jnp.float32)
    return (lines == place).astype(jnp.float32).astype(jnp.bfloat16)


def decode_place(ids, step_rows, slots, turned):
    step_of = lax.broadcasted_iota(jnp.int32, ids.shape, 1) // step_rows
    within = (step_of * DCAP).astype(jnp.float32) + count_before(ids, step_rows)
    return (turned * slots).astype(jnp.float32) + within


def greet_peers(own_group, own_dp, groups):
    barrier = pltpu.get_barrier_semaphore()
    for step in range(1, groups):
        pl.semaphore_signal(
            barrier,
            inc=1,
            device_id={"group": lax.rem(own_group + step, groups), "dp": own_dp},
            device_id_type=MESH,
        )
    pl.semaphore_signal(
        barrier, inc=1, device_id={"group": own_group, "dp": 1 - own_dp}, device_id_type=MESH
    )
    twin = own_group + 1 - 2 * lax.rem(own_group, 2)
    pl.semaphore_signal(
        barrier, inc=1, device_id={"group": twin, "dp": 1 - own_dp}, device_id_type=MESH
    )


def await_peers(groups):
    pl.semaphore_wait(pltpu.get_barrier_semaphore(), groups + 1)


def learner_kernel(
    groups,
    step_rows,
    tok,
    cot,
    scale_line,
    routes,
    dtok,
    droutes,
    master,
    grads_out,
    drows_out,
    grads,
    rounded,
    gate_scale,
    sel,
    far_sel,
    dsel,
    raw,
    far_raw,
    ids_out,
    ids_in,
    packed,
    far_packed,
    rows,
    dpacked,
    drows,
    weights,
    pre,
    left,
    raw_send,
    raw_recv,
    ids_send,
    ids_recv,
    near_send,
    near_recv,
    far_send,
    far_recv,
    side_send,
    side_recv,
    far_side_send,
    far_side_recv,
    dnear_send,
    dnear_recv,
    dhalf_send,
    dhalf_recv,
    out_sem,
    grads_sem,
):
    group = lax.axis_index("group")
    dp = lax.axis_index("dp")
    half = group // EXPERTS
    expert = lax.rem(group, EXPERTS)
    count, width = tok.shape
    hidden = weights.shape[0]
    tile = pick_tile(width)
    block = 2 * CAP
    chunk = EXPERTS * block
    piece = width // PIECES
    spans = [pl.ds(index * piece, piece) for index in range(PIECES)]

    def remote(src, dst, send, recv, to_group, to_dp):
        return pltpu.make_async_remote_copy(
            src_ref=src,
            dst_ref=dst,
            send_sem=send,
            recv_sem=recv,
            device_id={"group": to_group, "dp": to_dp},
            device_id_type=MESH,
        )

    def slots_of(ids):
        place = (ids * block).astype(jnp.float32) + count_before(ids, count)
        return one_hot_rows(chunk, jnp.concatenate([place, place + CAP], 1))

    greet_peers(group, dp, groups)
    gate_scale[...] = as_column(scale_line[...])
    ids_out[...] = jnp.broadcast_to(routes[...].astype(jnp.float32), ids_out.shape).astype(
        jnp.bfloat16
    )
    raw[:count] = tok[...]

    @pl.loop(0, width // tile)
    def _(index):
        columns = pl.ds(pl.multiple_of(index * tile, tile), tile)
        raw[count:, columns] = (gate_scale[...] * cot[:, columns].astype(jnp.float32)).astype(
            jnp.bfloat16
        )

    await_peers(groups)
    other_group = (1 - half) * EXPERTS + expert
    ids_copy = remote(ids_out, ids_in, ids_send, ids_recv, other_group, dp)
    ids_copy.start()
    across = [
        remote(
            raw.at[:, spans[index]],
            far_raw.at[:, spans[index]],
            raw_send.at[index],
            raw_recv.at[index],
            other_group,
            dp,
        )
        for index in range(PIECES)
    ]
    for copy in across:
        copy.start()

    sel[...] = slots_of(routes[...])

    @pl.loop(0, width // tile)
    def _(index):
        columns = pl.ds(pl.multiple_of(index * tile, tile), tile)
        picked = jnp.dot(sel[...], raw[:, columns], preferred_element_type=jnp.float32)
        packed[:, :, columns] = picked.astype(jnp.bfloat16).reshape(EXPERTS, block, tile)

    def peer(step):
        return half * EXPERTS + lax.rem(expert + step, EXPERTS)

    near = [None] + [
        remote(
            packed.at[lax.rem(expert + step, EXPERTS)],
            rows.at[0, 0, step],
            near_send.at[step],
            near_recv.at[step],
            peer(step),
            dp,
        )
        for step in range(1, EXPERTS)
    ]
    beside = [
        remote(
            packed.at[expert] if step == 0 else rows.at[0, 0, step],
            rows.at[1, 0, step],
            side_send.at[step],
            side_recv.at[step],
            group,
            1 - dp,
        )
        for step in range(EXPERTS)
    ]
    far_near = {}
    further = {}
    for index in range(PIECES):
        for step in range(EXPERTS):
            if step:
                far_near[index, step] = remote(
                    far_packed.at[lax.rem(expert + step, EXPERTS), :, spans[index]],
                    rows.at[0, 1, step, :, spans[index]],
                    far_send.at[index, step],
                    far_recv.at[index, step],
                    peer(step),
                    dp,
                )
            further[index, step] = remote(
                rows.at[0, 1, step, :, spans[index]],
                rows.at[1, 1, step, :, spans[index]],
                far_side_send.at[index, step],
                far_side_recv.at[index, step],
                group,
                1 - dp,
            )
    dnear = [None] + [
        remote(
            dpacked.at[lax.rem(expert + step, EXPERTS)],
            drows.at[0, step],
            dnear_send.at[step],
            dnear_recv.at[step],
            peer(step),
            dp,
        )
        for step in range(1, EXPERTS)
    ]
    dacross = [
        remote(
            dpacked.at[lax.rem(expert + step, EXPERTS)],
            drows.at[1, step],
            dhalf_send.at[step],
            dhalf_recv.at[step],
            (1 - half) * EXPERTS + lax.rem(expert + step, EXPERTS),
            dp,
        )
        for step in range(EXPERTS)
    ]

    twin = jnp.where(lax.rem(expert, 2) == 0, 1, EXPERTS - 1)
    mirror = EXPERTS - twin
    beside[0].start()
    remote(
        packed.at[lax.rem(expert + twin, EXPERTS)],
        rows.at[1, 0, twin],
        side_send.at[mirror],
        side_recv.at[twin],
        peer(twin),
        1 - dp,
    ).start()
    for step in range(1, EXPERTS):
        near[step].start()
    rows[0, 0, 0] = packed[expert]

    slots = dpacked.shape[1]
    ids = in_line(droutes)
    dsel[...] = one_hot_rows(EXPERTS * slots, decode_place(ids, step_rows, slots, ids))

    @pl.loop(0, width // tile)
    def _(index):
        columns = pl.ds(pl.multiple_of(index * tile, tile), tile)
        picked = jnp.dot(dsel[...], dtok[:, columns], preferred_element_type=jnp.float32)
        dpacked[:, :, columns] = picked.astype(jnp.bfloat16).reshape(EXPERTS, -1, tile)

    drows[0, 0] = dpacked[expert]
    lines = min(16, hidden)

    def cast_body(source):
        begin = pl.multiple_of(pl.program_id(0) * lines, lines)
        weights[pl.ds(begin, lines), :] = source[...].astype(jnp.bfloat16)

    pltpu.emit_pipeline(
        cast_body,
        grid=(hidden // lines,),
        in_specs=[pl.BlockSpec((lines, 3 * width), lambda i: (i, 0))],
        out_specs=[],
    )(master)

    near[1].wait_recv()
    near[EXPERTS - 1].wait_recv()
    remote(
        rows.at[0, 0, twin],
        rows.at[1, 0, twin],
        side_send.at[twin],
        side_recv.at[twin],
        group,
        1 - dp,
    ).start()
    for step in range(2, EXPERTS - 1):
        near[step].wait_recv()
        beside[step].start()

    def score(own, start, size):
        operand = own[:, :, pl.ds(start, size)].reshape(chunk, size)
        for part in range(3):
            pre[:, part * hidden : (part + 1) * hidden] += lax.dot_general(
                operand,
                weights[:, pl.ds(pl.multiple_of(part * width + start, 128), size)],
                CONTRACT_MINOR,
                preferred_element_type=jnp.float32,
            )

    def score_all(own):
        pre[...] = jnp.zeros_like(pre)

        @pl.loop(0, width // tile)
        def _(index):
            score(own, pl.multiple_of(index * tile, tile), tile)

    def accumulate(own, first=False, last=False):
        parts = pre[...].reshape(EXPERTS, block, 3 * hidden)
        gate_pre = parts[:, :CAP, :hidden]
        up_pre = parts[:, :CAP, hidden : 2 * hidden]
        back_pre = parts[:, CAP:, 2 * hidden :]
        silu_val, silu_grad = silu_parts(gate_pre)
        zeros = jnp.zeros_like(gate_pre)
        top = jnp.concatenate([back_pre * up_pre * silu_grad, back_pre * silu_val, zeros], 2)
        bottom = jnp.concatenate([zeros, zeros, silu_val * up_pre], 2)
        left[...] = (
            jnp.concatenate([top, bottom], 1)
            .reshape(chunk, 3 * hidden)
            .T.astype(jnp.bfloat16)
        )

        @pl.loop(0, width // tile)
        def _(index):
            columns = pl.ds(pl.multiple_of(index * tile, tile), tile)
            operand = own[:, :, columns].reshape(chunk, tile)
            value = jnp.dot(left[...], operand, preferred_element_type=jnp.float32)
            if first:
                grads[:, columns] = value
            elif last:
                rounded[:, columns] = (grads[:, columns] + value).astype(jnp.bfloat16)
                pltpu.make_async_copy(
                    rounded.at[:, columns], grads_out.at[:, columns], grads_sem.at[index]
                ).start()
            else:
                grads[:, columns] += value

    def spread(index):
        across[index].wait_recv()
        if index == 0:
            ids_copy.wait_recv()
            far_sel[...] = slots_of(ids_in[0:1, :].astype(jnp.float32).astype(jnp.int32))
        picked = jnp.dot(
            far_sel[...], far_raw[:, spans[index]], preferred_element_type=jnp.float32
        )
        far_packed[:, :, spans[index]] = picked.astype(jnp.bfloat16).reshape(
            EXPERTS, block, piece
        )
        for step in range(1, EXPERTS):
            far_near[index, step].start()
        rows[0, 1, 0, :, spans[index]] = far_packed[expert, :, spans[index]]
        further[index, 0].start()

    def pass_on(index):
        for step in range(1, EXPERTS):
            far_near[index, step].wait_recv()
            further[index, step].start()

    spread(0)
    own = rows.at[0, 0]
    score_all(own)
    accumulate(own, first=True)
    pass_on(0)
    for index in range(1, PIECES):
        spread(index)
        if index == PIECES - 1:
            for step in range(EXPERTS):
                dacross[step].start()
            for step in range(1, EXPERTS):
                dnear[step].start()
        pass_on(index)
    own = rows.at[0, 1]
    score_all(own)
    accumulate(own)
    for step in range(EXPERTS):
        beside[step].wait_recv()
    own = rows.at[1, 0]
    score_all(own)
    accumulate(own)
    own = rows.at[1, 1]
    pre[...] = jnp.zeros_like(pre)
    for index in range(PIECES):
        for step in range(EXPERTS):
            further[index, step].wait_recv()
        score(own, index * piece, piece)
    accumulate(own, last=True)
    for step in range(EXPERTS):
        dacross[step].wait_recv()
        if step:
            dnear[step].wait_recv()
    leave = pltpu.make_async_copy(drows, drows_out, out_sem)
    leave.start()

    @pl.loop(0, width // tile)
    def _(index):
        columns = pl.ds(pl.multiple_of(index * tile, tile), tile)
        pltpu.make_async_copy(
            rounded.at[:, columns], grads_out.at[:, columns], grads_sem.at[index]
        ).wait()

    leave.wait()
    ids_copy.wait_send()
    for copy in across + beside + near[1:] + dnear[1:] + dacross:
        copy.wait_send()
    for copy in far_near.values():
        copy.wait_send()
    for copy in further.values():
        copy.wait_send()


def decode_kernel(
    groups,
    step_rows,
    drows_in,
    roll_in,
    droutes,
    dscale,
    out,
    drows,
    roll,
    pre,
    own,
    side_out,
    side_in,
    back_out,
    back_in,
    side_send,
    side_recv,
    back_send,
    back_recv,
    in_sem,
):
    group = lax.axis_index("group")
    dp = lax.axis_index("dp")
    half = group // EXPERTS
    expert = lax.rem(group, EXPERTS)
    hidden, wide = roll.shape
    width = wide // 3
    out_width = width // 2
    tile = pick_tile(width)
    slots = drows.shape[0] // (2 * EXPERTS)
    pieces = side_out.shape[0]
    per_piece = 2 * EXPERTS // pieces
    fetches = [
        pltpu.make_async_copy(drows_in, drows, in_sem.at[0]),
        pltpu.make_async_copy(
            roll_in.at[:, : 2 * width], roll.at[:, : 2 * width], in_sem.at[1]
        ),
        pltpu.make_async_copy(
            roll_in.at[:, 2 * width :], roll.at[:, 2 * width :], in_sem.at[2]
        ),
    ]
    for fetch in fetches:
        fetch.start()
    greet_peers(group, dp, groups)
    pre[...] = jnp.zeros_like(pre)
    fetches[0].wait()
    fetches[1].wait()

    @pl.loop(0, width // tile)
    def _(index):
        start = pl.multiple_of(index * tile, tile)
        operand = drows[:, pl.ds(start, tile)]
        for part in range(2):
            begin = pl.multiple_of(part * width + start, 128)
            pre[:, part * hidden : (part + 1) * hidden] += lax.dot_general(
                operand,
                roll[:, pl.ds(begin, tile)],
                CONTRACT_MINOR,
                preferred_element_type=jnp.float32,
            )

    dec_silu, unused_grad = silu_parts(pre[:, :hidden])
    act = (dec_silu * pre[:, hidden:]).astype(jnp.bfloat16)
    fetches[2].wait()
    strip = 256 if out_width % 256 == 0 else 128
    for index in range(out_width // strip):
        begin = pl.multiple_of(2 * width + (1 - dp) * out_width + index * strip, 128)
        value = jnp.dot(act, roll[:, pl.ds(begin, strip)], preferred_element_type=jnp.float32)
        side_out[:, :, index * strip : (index + 1) * strip] = value.astype(jnp.bfloat16).reshape(
            pieces, -1, strip
        )
    order = list(range(pieces // 2, pieces)) + list(range(pieces // 2))
    side = [
        pltpu.make_async_remote_copy(
            src_ref=side_out.at[piece],
            dst_ref=side_in.at[piece],
            send_sem=side_send.at[piece],
            recv_sem=side_recv.at[piece],
            device_id={"group": group, "dp": 1 - dp},
            device_id_type=MESH,
        )
        for piece in range(pieces)
    ]
    await_peers(groups)
    for piece in order:
        side[piece].start()
    for index in range(out_width // strip):
        begin = pl.multiple_of(2 * width + dp * out_width + index * strip, 128)
        value = jnp.dot(act, roll[:, pl.ds(begin, strip)], preferred_element_type=jnp.float32)
        own[:, :, index * strip : (index + 1) * strip] = value.reshape(pieces, -1, strip)
    back = {}
    for piece in order:
        side[piece].wait_recv()
        total = (own[piece] + side_in[piece].astype(jnp.float32)).astype(jnp.bfloat16)
        total = total.reshape(per_piece, slots, out_width)
        for place in range(per_piece):
            far, step = divmod(piece * per_piece + place, EXPERTS)
            if far == 0 and step == 0:
                back_in[0, 0] = total[place]
                continue
            back_out[far, step] = total[place]
            to_half = 1 - half if far else half
            back[far, step] = pltpu.make_async_remote_copy(
                src_ref=back_out.at[far, step],
                dst_ref=back_in.at[far, step],
                send_sem=back_send.at[far, step],
                recv_sem=back_recv.at[far, step],
                device_id={
                    "group": to_half * EXPERTS + lax.rem(expert + EXPERTS - step, EXPERTS),
                    "dp": dp,
                },
                device_id_type=MESH,
            )
            back[far, step].start()
    for copy in back.values():
        copy.wait_recv()
    total = (back_in[0].astype(jnp.float32) + back_in[1].astype(jnp.float32)).astype(jnp.bfloat16)
    total = total.reshape(EXPERTS * slots, out_width)
    ids = in_line(droutes)
    turned = jnp.where(ids < expert, ids + EXPERTS - expert, ids - expert)
    back_sel = one_hot_rows(EXPERTS * slots, decode_place(ids, step_rows, slots, turned))
    picked = lax.dot_general(
        back_sel, total, CONTRACT_MAJOR, preferred_element_type=jnp.float32
    )
    out[...] = (as_column(in_line(dscale)) * picked).astype(jnp.bfloat16)
    for copy in back.values():
        copy.wait_send()
    for copy in side:
        copy.wait_send()


def adam_kernel(grads, master, first, second, new_master, new_first, new_second, roll):
    grad = grads[...].astype(jnp.float32)
    moment = beta_one * first[...] + (1.0 - beta_one) * grad
    square = beta_two * second[...] + (1.0 - beta_two) * grad * grad
    scale_one = adam_lr / (1.0 - beta_one**step_count)
    scale_two = 1.0 / (1.0 - beta_two**step_count)
    corrected = square * scale_two
    root = corrected * lax.rsqrt(corrected) + adam_eps
    value = (1.0 - adam_lr * decay_rate) * master[...] - (scale_one * moment) / root
    new_first[...] = moment
    new_second[...] = square
    new_master[...] = value
    roll[...] = value.astype(jnp.bfloat16)


def moved_rows(
    tokens,
    routes,
    gate_scale,
    cotangent,
    master,
    moment_one,
    moment_two,
    dec_tokens,
    dec_routes,
    dec_scale,
):
    groups = lax.axis_size("group")
    width = tokens.shape[1]
    hidden = master.shape[1]
    steps, dec_here = dec_tokens.shape[:2]
    slots = steps * DCAP
    tokens_here = tokens.shape[0]
    dec_line = jnp.transpose(dec_routes, (0, 2, 1))
    master_rows = master[0]
    vmem = pl.BlockSpec(memory_space=pltpu.VMEM)
    anywhere = pl.BlockSpec(memory_space=pl.ANY)
    dma = pltpu.SemaphoreType.DMA
    rows_all = 2 * 2 * EXPERTS * 2 * CAP
    grads, drows = pl.pallas_call(
        functools.partial(learner_kernel, groups, dec_here),
        out_shape=(
            jax.ShapeDtypeStruct((3 * hidden, width), jnp.bfloat16),
            jax.ShapeDtypeStruct((2, EXPERTS, slots, width), jnp.bfloat16),
        ),
        in_specs=[vmem] * 6 + [anywhere],
        out_specs=(anywhere, anywhere),
        scratch_shapes=[
            pltpu.VMEM((3 * hidden, width), jnp.float32),
            pltpu.VMEM((3 * hidden, width), jnp.bfloat16),
            pltpu.VMEM((tokens_here, 1), jnp.float32),
            pltpu.VMEM((EXPERTS * 2 * CAP, 2 * tokens_here), jnp.bfloat16),
            pltpu.VMEM((EXPERTS * 2 * CAP, 2 * tokens_here), jnp.bfloat16),
            pltpu.VMEM((EXPERTS * slots, steps * dec_here), jnp.bfloat16),
            pltpu.VMEM((2 * tokens_here, width), jnp.bfloat16),
            pltpu.VMEM((2 * tokens_here, width), jnp.bfloat16),
            pltpu.VMEM((16, tokens_here), jnp.bfloat16),
            pltpu.VMEM((16, tokens_here), jnp.bfloat16),
            pltpu.VMEM((EXPERTS, 2 * CAP, width), jnp.bfloat16),
            pltpu.VMEM((EXPERTS, 2 * CAP, width), jnp.bfloat16),
            pltpu.VMEM((2, 2, EXPERTS, 2 * CAP, width), jnp.bfloat16),
            pltpu.VMEM((EXPERTS, slots, width), jnp.bfloat16),
            pltpu.VMEM((2, EXPERTS, slots, width), jnp.bfloat16),
            pltpu.VMEM((hidden, 3 * width), jnp.bfloat16),
            pltpu.VMEM((EXPERTS * 2 * CAP, 3 * hidden), jnp.float32),
            pltpu.VMEM((3 * hidden, EXPERTS * 2 * CAP), jnp.bfloat16),
            dma((PIECES,)),
            dma((PIECES,)),
            dma(()),
            dma(()),
            dma((EXPERTS,)),
            dma((EXPERTS,)),
            dma((PIECES, EXPERTS)),
            dma((PIECES, EXPERTS)),
            dma((EXPERTS,)),
            dma((EXPERTS,)),
            dma((PIECES, EXPERTS)),
            dma((PIECES, EXPERTS)),
            dma((EXPERTS,)),
            dma((EXPERTS,)),
            dma((EXPERTS,)),
            dma((EXPERTS,)),
            dma(()),
            dma((width // pick_tile(width),)),
        ],
        compiler_params=pltpu.CompilerParams(
            collective_id=0, has_side_effects=True, vmem_limit_bytes=56 * 2**20
        ),
        cost_estimate=pl.CostEstimate(
            flops=12 * rows_all * hidden * width,
            bytes_accessed=24 * hidden * width,
            transcendentals=rows_all * hidden,
        ),
        name="learner",
    )(
        tokens,
        cotangent,
        gate_scale.reshape(1, tokens_here),
        routes.reshape(1, tokens_here),
        dec_tokens.reshape(steps * dec_here, width),
        dec_line,
        master_rows,
    )
    lines = min(32, hidden)
    tall = hidden // lines
    block = pl.BlockSpec((lines, width), lambda line, part: (line, part))
    wide = jax.ShapeDtypeStruct((hidden, 3 * width), jnp.float32)
    master_new, moment_new, second_new, rollout = pl.pallas_call(
        adam_kernel,
        grid=(tall, 3),
        out_shape=(wide, wide, wide, jax.ShapeDtypeStruct(wide.shape, jnp.bfloat16)),
        in_specs=[
            pl.BlockSpec((lines, width), lambda line, part: (part * tall + line, 0)),
            block,
            block,
            block,
        ],
        out_specs=(block, block, block, block),
        compiler_params=pltpu.CompilerParams(vmem_limit_bytes=56 * 2**20),
        cost_estimate=pl.CostEstimate(
            flops=60 * hidden * width,
            bytes_accessed=90 * hidden * width,
            transcendentals=6 * hidden * width,
        ),
        name="adam",
    )(grads, master_rows, moment_one[0], moment_two[0])
    out_width = width // 2
    rows_dec = 2 * EXPERTS * slots
    pieces = 8
    dec_out = pl.pallas_call(
        functools.partial(decode_kernel, groups, dec_here),
        out_shape=jax.ShapeDtypeStruct((steps * dec_here, out_width), jnp.bfloat16),
        in_specs=[anywhere, anywhere, vmem, vmem],
        out_specs=vmem,
        scratch_shapes=[
            pltpu.VMEM((rows_dec, width), jnp.bfloat16),
            pltpu.VMEM((hidden, 3 * width), jnp.bfloat16),
            pltpu.VMEM((rows_dec, 2 * hidden), jnp.float32),
            pltpu.VMEM((pieces, rows_dec // pieces, out_width), jnp.float32),
            pltpu.VMEM((pieces, rows_dec // pieces, out_width), jnp.bfloat16),
            pltpu.VMEM((pieces, rows_dec // pieces, out_width), jnp.bfloat16),
            pltpu.VMEM((2, EXPERTS, slots, out_width), jnp.bfloat16),
            pltpu.VMEM((2, EXPERTS, slots, out_width), jnp.bfloat16),
            dma((pieces,)),
            dma((pieces,)),
            dma((2, EXPERTS)),
            dma((2, EXPERTS)),
            dma((3,)),
        ],
        compiler_params=pltpu.CompilerParams(
            collective_id=1, has_side_effects=True, vmem_limit_bytes=56 * 2**20
        ),
        cost_estimate=pl.CostEstimate(
            flops=6 * rows_dec * hidden * width,
            bytes_accessed=6 * hidden * width,
            transcendentals=rows_dec * hidden,
        ),
        name="decode",
    )(
        drows.reshape(rows_dec, width),
        rollout,
        dec_line,
        jnp.transpose(dec_scale, (0, 2, 1)),
    )
    return (
        master_new[None],
        moment_new[None],
        second_new[None],
        dec_out.reshape(steps, dec_here, out_width),
    )


def solution(mesh):
    in_specs = (
        P(("group", "dp"), None),
        P(("group", "dp"), None),
        P(("group", "dp"), None),
        P(("group", "dp"), None),
        P("group", "dp", None),
        P("group", "dp", None),
        P("group", "dp", None),
        P(None, "group", None),
        P(None, "group", None),
        P(None, "group", None),
    )
    out_specs = (
        P("group", "dp", None),
        P("group", "dp", None),
        P("group", "dp", None),
        P(None, "group", "dp"),
    )
    in_place = mesh.shape["group"] == 2 * EXPERTS and mesh.shape["dp"] == 2
    body = moved_rows if in_place else shards
    return jax.shard_map(body, mesh=mesh, in_specs=in_specs, out_specs=out_specs, check_vma=False)
```
